32 devices in a mesh: parts: 2 (over y), blk: 4 (over z), chan: 2 (over x), freq: 2 (over core).
Axes of the slice: x: 2, y: 2, z: 4, core: 2. Of those that a mesh axis runs over, the one named last changes fastest.
Arguments:
- records: bfloat16 [128, 2, 512, 1024], P(('parts', 'blk'), None, 'freq', 'chan'), parts along dimension 0, may hold values from -6 to 6
- templates: bfloat16 [4, 2, 512, 1024], P('blk', None, 'freq', 'chan'), may hold values from -0.125 to 0.125
- masks: int32 [4, 4], replicated, may hold values 0 or 1
- offsets: int32 [4], replicated, may hold values from 0 to 1023
Outputs:
- correlation: float32 [4, 128, 1024], P(None, ('parts', 'blk'), ('chan', 'freq')), parts along dimension 1
The draws below stay inside these ranges and needn't reach their ends.
There are 2 independent parts, one for each index of `parts`. The reference program is written for one: setup_inputs(seed, part) draws one part's arguments, and reference() takes and returns one part's arrays. A program takes and returns all parts, laid end to end along the dimension named above; an argument that names none is the same for every part. Nothing has to cross between parts.
All inputs are finite; a program needn't handle non-finite values.
Results may differ from the reference program's by a relative error of at most 0.0003.
Values may be sent and summed in bfloat16 or wider, within the bound.
No kernel may reach another device: no remote copies, remote signals or barrier semaphores. Data moves between devices by JAX's collectives and lax.ppermute only.
A program may use at most 64 MiB of HBM per device.

```python
import math
import jax
import jax.numpy as jnp
from jax import lax

NSAMP = 1024
BINS = 512
CB = 256
APER_BLOCKS = 4
CH = 1024
W_DEV = 16
TEMPL = 4
WINDOWS = 64
N_BLK = 4


def with_ends(values, rng, smallest, high):
    longest = values.shape.index(max(values.shape))
    spots = []
    for shift in (0, 1):
        where = [jax.random.randint(jax.random.fold_in(rng, axis), (), 0, length) for axis, length in enumerate(values.shape)]
        where[longest] = (where[longest] + shift) % values.shape[longest]
        spots.append(tuple(where))
    return values.at[spots[0]].set(smallest).at[spots[1]].set(high)


def levels(stream_key, extent, split, least, largest):
    level = 1.0
    for dim, shards_of in split:
        steps = jax.random.uniform(jax.random.fold_in(jax.random.fold_in(stream_key, 6), dim), (shards_of,), jnp.float32, least / len(split), largest / len(split))
        level = level * jnp.repeat(jnp.exp(steps), extent[dim] // shards_of).reshape((-1,) + (1,) * (len(extent) - 1 - dim))
    return level


def bell_draw(rng, extent, deviation, limit, pieces=(), held_as=jnp.bfloat16):
    drawn = deviation * jax.random.normal(rng, extent, jnp.float32)
    if pieces:
        drawn = drawn * levels(rng, extent, pieces, -0.22, 0.18)
    return jnp.clip(drawn, -limit, limit).astype(held_as)


def setup_inputs(seed: int = 0, part: int = 0) -> dict:
    splits = jax.random.split(jax.random.key(seed), 5)
    part_splits = jax.random.split(jax.random.fold_in(splits[4], part), 5)
    records = bell_draw(part_splits[0], (WINDOWS, 2, BINS, CH), 1.0, 6.0, ((0, 4), (2, 2), (3, 2)))
    templates = bell_draw(splits[1], (TEMPL, 2, BINS, CH), (2 * CH) ** -0.5, 0.125, ((0, 4), (2, 2), (3, 2)))
    masks = with_ends((jax.random.randint(splits[2], (TEMPL, APER_BLOCKS), 0, 4) < 3).astype(jnp.int32), jax.random.fold_in(splits[2], 1), 0, 1)
    offsets = with_ends(jax.random.randint(splits[3], (TEMPL,), 0, NSAMP), jax.random.fold_in(splits[3], 1), 0, NSAMP - 1).astype(jnp.int32)
    return dict(records=records, templates=templates, masks=masks, offsets=offsets)


def rotate_spectra(real_part, imag_part, offsets):
    bin_index = lax.iota(jnp.int32, BINS)
    phase = offsets[:, None].astype(jnp.int32) * bin_index[None, :] % NSAMP
    angle = 2.0 * math.pi / NSAMP * phase.astype(jnp.float32)
    cosine = jnp.cos(angle)[:, None, :]
    sine_table = jnp.sin(angle)[:, None, :]
    return (real_part * cosine - imag_part * sine_table, real_part * sine_table + imag_part * cosine)

def reference(records, templates, masks, offsets):
    channel_mask = jnp.repeat(masks, CB, axis=1).astype(jnp.bfloat16)
    masked_templates = (templates * channel_mask[:, None, None, :]).astype(jnp.float32)
    window_blocks = records.reshape(N_BLK, W_DEV, 2, BINS, CH)

    def correlate_block(window_block):
        window_block = window_block.astype(jnp.float32)
        products = jnp.einsum('tpkc,wqkc->tpqwk', masked_templates, window_block, precision=lax.Precision.HIGHEST)
        real_part = products[:, 0, 0] + products[:, 1, 1]
        imag_part = products[:, 0, 1] - products[:, 1, 0]
        return (real_part, imag_part)
    real_part, imag_part = lax.map(correlate_block, window_blocks)
    real_part = jnp.transpose(real_part, (1, 0, 2, 3)).reshape(TEMPL, WINDOWS, BINS)
    imag_part = jnp.transpose(imag_part, (1, 0, 2, 3)).reshape(TEMPL, WINDOWS, BINS)
    rot_real, rot_imag = rotate_spectra(real_part, imag_part, offsets)
    bin_index = lax.iota(jnp.int32, BINS)
    lag_index = lax.iota(jnp.int32, NSAMP)
    phase = bin_index[:, None] * lag_index[None, :] % NSAMP
    angle = 2.0 * math.pi / NSAMP * phase.astype(jnp.float32)
    scale = math.sqrt(2.0 / BINS)
    first = jnp.einsum('twk,kn->twn', rot_real, jnp.cos(angle), precision=lax.Precision.HIGHEST)
    second = jnp.einsum('twk,kn->twn', rot_imag, jnp.sin(angle), precision=lax.Precision.HIGHEST)
    return scale * (first - second)
```

```python
import functools
import math

import jax
import jax.numpy as jnp
import numpy as np
from jax import lax
from jax.experimental import pallas as pl
from jax.experimental.pallas import tpu as pltpu
from jax.sharding import PartitionSpec as P

NSAMP = 1024
BINS = 512
SUB = 64
FOLD = 256


def lag_tables():
    bins = np.arange(BINS).reshape(-1, SUB)
    angle = 2.0 * math.pi / NSAMP * (bins[..., None] * np.arange(FOLD) % NSAMP)
    table = math.sqrt(2.0 / BINS) * np.concatenate([np.cos(angle), -np.sin(angle)], axis=1)
    table = table.astype(np.float32)
    high = table.astype(jnp.bfloat16)
    low = (table - high.astype(np.float32)).astype(jnp.bfloat16)
    return high, low


def two_halves(values):
    high = values.astype(jnp.bfloat16)
    return high, (values - high.astype(jnp.float32)).astype(jnp.bfloat16)


def product(left, right, contract):
    return lax.dot_general(left, right, ((contract[:1], contract[1:]), ((), ())), preferred_element_type=jnp.float32)


def lags_kernel(plan, n_masks, n_chan, at, records, turn, high, low, *rest):
    d, starts, n_before, others, blocks = plan
    pieces, rest = rest[: len(starts)], rest[len(starts) :]
    before, rest = rest[:n_before], rest[n_before:]
    finished, outs = rest[: len(others)], rest[len(others) :]
    windows, width = records.shape[0], records.shape[3]
    template_at = at[0] ^ d
    lane = lax.broadcasted_iota(jnp.int32, (1, width), 1)
    n_here = n_masks // n_chan
    mask = jnp.zeros((1, width), jnp.float32)
    for b in range(n_here):
        here = at[5 + template_at * n_masks + at[2] * n_here + b]
        mask = jnp.where(lane // (width // n_here) == b, here.astype(jnp.float32), mask)
    mask = mask.astype(jnp.bfloat16)
    row = lax.broadcasted_iota(jnp.int32, (2 * SUB, 2 * SUB), 0)
    lane = lax.broadcasted_iota(jnp.int32, (2 * SUB, 2 * SUB), 1)
    same_bin = row % SUB == lane % SUB
    pairs = windows // 2
    order = [w for v in range(pairs) for w in (v, v + pairs)]
    real_lane = lax.broadcasted_iota(jnp.int32, (windows, 2 * SUB), 1) < SUB
    straight, turned, tables = [], [], []
    for piece, (fixed, moved) in zip(pieces, starts):
        for sub in range(piece.shape[2] // SUB):
            run = fixed // SUB + sub + (at[3] * (moved // SUB) if moved else 0)
            bins = pl.ds(pl.multiple_of(run * SUB, SUB), SUB)
            first, second = (piece[0, part, sub * SUB : (sub + 1) * SUB, :] * mask for part in range(2))
            weights = jnp.concatenate(
                [jnp.concatenate([first, second], axis=1), jnp.concatenate([-second, first], axis=1)], axis=0
            )
            rows = jnp.concatenate(
                [jnp.concatenate([records[w, 0, bins, :], records[w, 1, bins, :]], axis=1) for w in order], axis=0
            )
            every = product(weights, rows, (1, 1))
            every = [jnp.where(same_bin, every[:, v * 2 * SUB : (v + 1) * 2 * SUB], 0.0) for v in range(pairs)]
            real = jnp.concatenate([jnp.sum(e[:SUB], axis=0, keepdims=True) for e in every], axis=0)
            imag = jnp.concatenate([jnp.sum(e[SUB:], axis=0, keepdims=True) for e in every], axis=0)
            real = jnp.concatenate([real, pltpu.roll(real, SUB, 1)], axis=0)
            imag = jnp.concatenate([pltpu.roll(imag, SUB, 1), imag], axis=0)
            spectrum = jnp.where(real_lane, real, imag)
            cosine, sine_table = (turn[template_at, i, pl.ds(run, 1)] for i in range(2))
            spectrum = spectrum * cosine + pltpu.roll(spectrum, SUB, 1) * sine_table
            straight.append(spectrum)
            turned.append(jnp.where(real_lane, 1.0, -1.0) * pltpu.roll(spectrum, SUB, 1))
            tables.append(at[1] + run)
    straight, turned = (jnp.concatenate(s, axis=1) for s in (straight, turned))
    lane = lax.broadcasted_iota(jnp.int32, straight.shape, 1) % 4
    picked = [jnp.where(lane == r, straight, 0.0) for r in range(4)]
    picked += [jnp.where(lane == r, turned, 0.0) for r in (1, 3)]
    rows = jnp.concatenate(picked, axis=0)
    rows_high, rows_low = two_halves(rows)
    table_high, table_low = (jnp.concatenate([t[run] for run in tables], axis=0) for t in (high, low))
    both = product(jnp.concatenate([rows_high, rows_low], axis=0), table_high, (1, 0))
    sums = both[: rows.shape[0]] + both[rows.shape[0] :] + product(rows_high, table_low, (1, 0))
    re0, re1, re2, re3, im1, im3 = (sums[i * windows : (i + 1) * windows] for i in range(6))
    even, odd, even_turned, odd_turned = re0 + re2, re1 + re3, re0 - re2, im1 - im3
    found = jnp.concatenate([even + odd, even_turned - odd_turned, even - odd, even_turned + odd_turned], axis=1)
    for b in before:
        found += b[...]
    if blocks is None:
        outs[0][...] = found
        return
    *outs, lags = outs
    block = lags.shape[2]
    for i, whole in enumerate([other[...] for other in finished] + [found]):
        for n in range(blocks):
            lags[n] = whole[:, n * block : (n + 1) * block]
        for n in range(blocks):
            outs[n][i] = lags[at[4] ^ n]


def template_lags(split, at, held, d, pieces, before=(), others=None, blocks=None):
    records = held[0]
    windows = records.shape[0]
    starts = tuple(start for _, start in pieces)
    plan = (d, starts, len(before), others or (), None if others is None else blocks)
    whole = pl.BlockSpec(memory_space=pltpu.VMEM)
    if others is None:
        out_shape = [jax.ShapeDtypeStruct((windows, NSAMP), jnp.float32)]
        scratch = []
    else:
        block = (windows, NSAMP // blocks)
        out_shape = [jax.ShapeDtypeStruct((len(others) + 1,) + block, jnp.float32)] * blocks
        scratch = [pltpu.VMEM((blocks,) + block, jnp.float32)]
    operands = (*held, *(piece for piece, _ in pieces), *before, *(others or ()))
    return pl.pallas_call(
        functools.partial(lags_kernel, plan, *split),
        in_specs=[pl.BlockSpec(memory_space=pltpu.SMEM)] + [whole] * len(operands),
        out_specs=[whole] * len(out_shape),
        out_shape=out_shape,
        scratch_shapes=scratch,
        compiler_params=pltpu.CompilerParams(vmem_limit_bytes=24 * 2**20),
    )(at, *operands)


def sum_kernel(orders, at, *refs):
    *parts, out = refs
    per = len(parts) // len(orders)
    for g, order in enumerate(orders):
        for i, d in enumerate(order):
            total = parts[g * per][i]
            for part in parts[g * per + 1 : (g + 1) * per]:
                total += part[i]
            out[at[0] ^ d] = total


def partners(n, d):
    return [(i, i ^ d) for i in range(n)]


def after(value, *others):
    return lax.optimization_barrier((value,) + others)[0]


def shards(records, templates, masks, offsets):
    n_blk, n_chan, n_freq, n_parts = (lax.axis_size(a) for a in ("blk", "chan", "freq", "parts"))
    blk_at, chan_at, freq_at, part_at = (lax.axis_index(a) for a in ("blk", "chan", "freq", "parts"))
    windows, _, bin_count, width = records.shape
    runs = bin_count // SUB
    blocks = n_chan * n_freq
    split = (masks.shape[1], n_chan)
    at = jnp.concatenate(
        [
            jnp.stack([blk_at, freq_at * runs, chan_at, part_at, chan_at * n_freq + freq_at]),
            masks.reshape(-1),
        ]
    ).astype(jnp.int32)
    bin_index = (freq_at * bin_count + lax.iota(jnp.int32, bin_count)).reshape(runs, 1, SUB)
    phase = offsets[:, None, None, None] * bin_index % NSAMP
    angle = 2.0 * math.pi / NSAMP * phase.astype(jnp.float32)
    cosine, sine_table = jnp.cos(angle), jnp.sin(angle)
    turn = jnp.stack(
        [jnp.concatenate([cosine, cosine], axis=2), jnp.concatenate([-sine_table, sine_table], axis=2)], axis=1
    ).reshape(offsets.shape[0], 2, runs, 2 * SUB)
    high, low = (jnp.asarray(t) for t in lag_tables())
    held = [pltpu.with_memory_space_constraint(a, pltpu.VMEM) for a in (records, turn, high, low)]

    def exchange(found):
        return [found[0]] + [lax.ppermute(found[n], ("chan", "freq"), partners(blocks, n)) for n in range(1, blocks)]

    half = bin_count // 2
    mine = lax.dynamic_slice_in_dim(templates, part_at * half, half, 2)
    swap = lambda a: lax.ppermute(a, "parts", partners(2, 1))
    far = sorted(range(2, n_blk), key=lambda d: -(d & -d))
    arrived = {d: lax.ppermute(mine, "blk", partners(n_blk, d)) for d in far}
    near = lax.ppermute(templates, "blk", partners(n_blk, 1))
    own = (0, half)
    other = (half, -half)
    found = {0: template_lags(split, at, held, 0, [(templates, (0, 0))])[0]}
    swapped = {}
    last = found[0]
    for d in far:
        swapped[d] = swap(after(arrived[d], last))
        last = template_lags(split, at, held, d, [(arrived[d], own)])[0]
        found[d] = last
    for d in far[:-1]:
        found[d] = template_lags(split, at, held, d, [(swapped[d], other)], before=[found[d]])[0]
    d = far[-1]
    ready = [e for e in found if e != d]
    first = exchange(template_lags(split, at, held, 1, [(near, (0, 0))], others=[found[e] for e in ready], blocks=blocks))
    last = exchange(template_lags(split, at, held, d, [(swapped[d], other)], before=[found[d]], others=[], blocks=blocks))
    return pl.pallas_call(
        functools.partial(sum_kernel, (ready + [1], [d])),
        in_specs=[pl.BlockSpec(memory_space=pltpu.SMEM)] + [pl.BlockSpec(memory_space=pltpu.VMEM)] * (2 * blocks),
        out_specs=pl.BlockSpec(memory_space=pltpu.VMEM),
        out_shape=jax.ShapeDtypeStruct((n_blk, windows, NSAMP // blocks), jnp.float32),
        compiler_params=pltpu.CompilerParams(vmem_limit_bytes=24 * 2**20),
    )(at, *first, *last)


def solution(mesh):
    placed = (P(("parts", "blk"), None, "freq", "chan"), P("blk", None, "freq", "chan"), P(), P())
    return jax.shard_map(
        shards,
        mesh=mesh,
        in_specs=placed,
        out_specs=P(None, ("parts", "blk"), ("chan", "freq")),
        check_vma=False,
    )
```

```python
import functools
import math

import jax
import jax.numpy as jnp
import numpy as np
from jax import lax
from jax.experimental import pallas as pl
from jax.experimental.pallas import tpu as pltpu
from jax.sharding import PartitionSpec as P

NSAMP = 1024
BINS = 512
SUB = 64
FOLD = 256
BATCH = 4
VMEM_LIMIT = 24 * 2**20


def lag_tables():
    bins = np.arange(BINS).reshape(-1, SUB)
    angle = 2.0 * math.pi / NSAMP * (bins[..., None] * np.arange(FOLD) % NSAMP)
    table = math.sqrt(2.0 / BINS) * np.concatenate([np.cos(angle), -np.sin(angle)], axis=1)
    table = table.astype(np.float32)
    high = table.astype(jnp.bfloat16)
    low = (table - high.astype(np.float32)).astype(jnp.bfloat16)
    return high, low


def two_halves(values):
    high = values.astype(jnp.bfloat16)
    return high, (values - high.astype(jnp.float32)).astype(jnp.bfloat16)


def product(left, right, contract):
    return lax.dot_general(left, right, ((contract[:1], contract[1:]), ((), ())), preferred_element_type=jnp.float32)


def mask_row(masks, template_at, width):
    here = masks.shape[1] // lax.axis_size("chan")
    first = lax.axis_index("chan") * here
    lane = lax.broadcasted_iota(jnp.int32, (1, width), 1) // (width // here)
    row = jnp.zeros((1, width), jnp.float32)
    for b in range(here):
        row = jnp.where(lane == b, masks[template_at, first + b].astype(jnp.float32), row)
    return row


def run_spectrum(template_at, run, piece, used, records, turn):
    windows, pairs = records.shape[0], records.shape[0] // 2
    bins = pl.ds(pl.multiple_of(run * SUB, SUB), SUB)
    mask = used[template_at].astype(jnp.bfloat16)
    first, second = piece[0] * mask, piece[1] * mask
    weights = jnp.concatenate(
        [jnp.concatenate([first, second], axis=1), jnp.concatenate([-second, first], axis=1)], axis=0
    )
    row = lax.broadcasted_iota(jnp.int32, (2 * SUB, 2 * SUB), 0)
    lane = lax.broadcasted_iota(jnp.int32, (2 * SUB, 2 * SUB), 1)
    same_bin = row % SUB == lane % SUB
    real, imag = [], []
    for v in range(pairs):
        rows = jnp.concatenate(
            [jnp.concatenate([records[w, 0, bins, :], records[w, 1, bins, :]], axis=1) for w in (v, v + pairs)], axis=0
        )
        every = jnp.where(same_bin, product(weights, rows, (1, 1)), 0.0)
        real.append(jnp.sum(every[:SUB], axis=0, keepdims=True))
        imag.append(jnp.sum(every[SUB:], axis=0, keepdims=True))
    real, imag = jnp.concatenate(real, axis=0), jnp.concatenate(imag, axis=0)
    real = jnp.concatenate([real, pltpu.roll(real, SUB, 1)], axis=0)
    imag = jnp.concatenate([pltpu.roll(imag, SUB, 1), imag], axis=0)
    real_lane = lax.broadcasted_iota(jnp.int32, (windows, 2 * SUB), 1) < SUB
    spectrum = jnp.where(real_lane, real, imag)
    cosine, sine_table = (turn[template_at, i, pl.ds(run, 1)] for i in range(2))
    return spectrum * cosine + pltpu.roll(spectrum, SUB, 1) * sine_table


def all_lags(spectra, high, low):
    runs, windows, width = spectra.shape
    real_lane = lax.broadcasted_iota(jnp.int32, (windows, width), 1) < SUB
    sign = jnp.where(real_lane, 1.0, -1.0)
    straight = jnp.concatenate([spectra[r] for r in range(runs)], axis=1)
    turned = jnp.concatenate([sign * pltpu.roll(spectra[r], SUB, 1) for r in range(runs)], axis=1)
    lane = lax.broadcasted_iota(jnp.int32, straight.shape, 1) % 4
    picked = [jnp.where(lane == r, straight, 0.0) for r in range(4)]
    picked += [jnp.where(lane == r, turned, 0.0) for r in (1, 3)]
    rows = jnp.concatenate(picked, axis=0)
    rows_high, rows_low = two_halves(rows)
    table_high, table_low = (jnp.concatenate([t[r] for r in range(runs)], axis=0) for t in (high, low))
    both = product(jnp.concatenate([rows_high, rows_low], axis=0), table_high, (1, 0))
    sums = both[: rows.shape[0]] + both[rows.shape[0] :] + product(rows_high, table_low, (1, 0))
    re0, re1, re2, re3, im1, im3 = (sums[i * windows : (i + 1) * windows] for i in range(6))
    even, odd, even_turned, odd_turned = re0 + re2, re1 + re3, re0 - re2, im1 - im3
    return [even + odd, even_turned - odd_turned, even - odd, even_turned + odd_turned]


def own_kernel(
    masks, offsets, records, templates, high, low, held, turn, used, held_high, held_low, spectra, template, numbers, sems
):
    runs = turn.shape[2]
    first_run = lax.axis_index("freq") * runs
    small = [
        pltpu.make_async_copy(masks, numbers[0], sems.at[0]),
        pltpu.make_async_copy(offsets, numbers[1], sems.at[1]),
    ]
    pieces = [
        pltpu.make_async_copy(values.at[:, :, pl.ds(r * SUB, SUB), :], to.at[:, :, pl.ds(r * SUB, SUB), :], sem)
        for r in range(runs)
        for values, to, sem in (
            (templates, template, sems.at[4 + 2 * r]),
            (records, held, sems.at[5 + 2 * r]),
        )
    ]
    tables = [
        pltpu.make_async_copy(table.at[pl.ds(first_run, runs)], to, sems.at[2 + i])
        for i, (table, to) in enumerate(((high, held_high), (low, held_low)))
    ]
    for copy in small + pieces + tables:
        copy.start()
    for copy in small:
        copy.wait()
    masks, offsets = numbers
    row = lax.broadcasted_iota(jnp.int32, (runs, 2 * SUB), 0)
    lane = lax.broadcasted_iota(jnp.int32, (runs, 2 * SUB), 1)
    bin_index = (first_run + row) * SUB + lane % SUB
    sign = jnp.where(lane < SUB, -1.0, 1.0)
    for t in range(turn.shape[0]):
        phase = offsets[t] * bin_index % NSAMP
        angle = 2.0 * math.pi / NSAMP * phase.astype(jnp.float32)
        turn[t, 0] = jnp.cos(angle)
        turn[t, 1] = jnp.sin(angle) * sign
        used[t] = mask_row(masks, t, held.shape[3])
    template_at = lax.axis_index("blk")
    for r in range(runs):
        for copy in pieces[2 * r : 2 * r + 2]:
            copy.wait()
        piece = template[0, :, r * SUB : (r + 1) * SUB, :]
        spectra[r] = run_spectrum(template_at, r, piece, used, held, turn)
    for copy in tables:
        copy.wait()


def piece_kernel(plan, held, turn, used, high, low, *rest):
    d, moved, whole = plan
    found = []
    if d is not None:
        piece, *rest = rest
        template_at = lax.axis_index("blk") ^ d
        first = lax.axis_index("parts") * moved[1] + moved[0]
        found = [
            run_spectrum(template_at, first + r, piece[0, :, r * SUB : (r + 1) * SUB, :], used, held, turn)
            for r in range(piece.shape[2] // SUB)
        ]
    if whole is None:
        for r, spectrum in enumerate(found):
            rest[0][r] = spectrum
        return
    n_in = sum(len(w) for w in whole)
    before, outs, (spectra, lags) = rest[:n_in], rest[n_in:-2], rest[-2:]
    at = 0
    for i, starts in enumerate(whole):
        for start, step in starts:
            run = lax.axis_index("parts") * step + start
            for r in range(before[at].shape[0]):
                spectra[i, run + r] = before[at][r]
            at += 1
    for r, spectrum in enumerate(found):
        spectra[len(whole) - 1, first + r] = spectrum
    me = lax.axis_index("chan") * lax.axis_size("freq") + lax.axis_index("freq")
    width = lags.shape[2]
    total = spectra.shape[0]
    for begin in range(0, total, BATCH):
        many = min(BATCH, total - begin)
        rows = jnp.concatenate([spectra[begin + i] for i in range(many)], axis=1)
        folded = all_lags(rows, high, low)
        for i in range(many):
            at = slice(i * held.shape[0], (i + 1) * held.shape[0])
            for n in range(len(outs)):
                start = n * width
                lags[n] = folded[start // FOLD][at, start % FOLD : start % FOLD + width]
            for n in range(len(outs)):
                outs[n][begin + i] = lags[me ^ n]


def sum_kernel(orders, *refs):
    *parts, out = refs
    per = len(parts) // len(orders)
    for g, order in enumerate(orders):
        for i, d in enumerate(order):
            total = parts[g * per][i]
            for part in parts[g * per + 1 : (g + 1) * per]:
                total += part[i]
            out[lax.axis_index("blk") ^ d] = total


IN_SMEM = pl.BlockSpec(memory_space=pltpu.SMEM)
IN_VMEM = pl.BlockSpec(memory_space=pltpu.VMEM)
IN_HBM = pl.BlockSpec(memory_space=pltpu.HBM)
PARAMS = pltpu.CompilerParams(vmem_limit_bytes=VMEM_LIMIT)


def in_vmem(values):
    return [pltpu.with_memory_space_constraint(v, pltpu.VMEM) for v in values]


def in_hbm(values):
    return [pltpu.with_memory_space_constraint(v, pltpu.HBM) for v in values]


def own_template(masks, offsets, records, template, high, low):
    windows, _, bin_count, width = records.shape
    runs = bin_count // SUB
    table = (runs,) + high.shape[1:]
    out_shape = [
        pltpu.VMEM(records.shape, records.dtype),
        pltpu.VMEM((offsets.shape[0], 2, runs, 2 * SUB), jnp.float32),
        pltpu.VMEM((offsets.shape[0], 1, width), jnp.float32),
        pltpu.VMEM(table, high.dtype),
        pltpu.VMEM(table, low.dtype),
        pltpu.VMEM((runs, windows, 2 * SUB), jnp.float32),
    ]
    *held, spectra = pl.pallas_call(
        own_kernel,
        in_specs=[IN_HBM] * 6,
        out_specs=[IN_VMEM] * len(out_shape),
        out_shape=out_shape,
        scratch_shapes=[
            pltpu.VMEM(template.shape, template.dtype),
            (pltpu.SMEM(masks.shape, masks.dtype), pltpu.SMEM(offsets.shape, offsets.dtype)),
            pltpu.SemaphoreType.DMA((2 * runs + 4,)),
        ],
        compiler_params=PARAMS,
    )(*in_hbm((masks, offsets, records, template, high, low)))
    return held, spectra


def add_piece(held, d, moved, piece):
    windows = held[0].shape[0]
    return pl.pallas_call(
        functools.partial(piece_kernel, (d, moved, None)),
        in_specs=[IN_VMEM] * 6,
        out_specs=IN_VMEM,
        out_shape=pltpu.VMEM((piece.shape[2] // SUB, windows, 2 * SUB), jnp.float32),
        compiler_params=PARAMS,
    )(*in_vmem(held), *in_vmem([piece]))


def transform(held, whole, blocks):
    return finish(held, None, None, None, whole, blocks)


def finish(held, d, moved, piece, whole, blocks):
    windows, _, bin_count, _ = held[0].shape
    block = (windows, NSAMP // blocks)
    before = [spectra for pieces in whole for spectra, _ in pieces]
    places = tuple(tuple(at for _, at in pieces) for pieces in whole)
    return pl.pallas_call(
        functools.partial(piece_kernel, (d, moved, places)),
        in_specs=[IN_VMEM] * (len(held) + (piece is not None) + len(before)),
        out_specs=[IN_VMEM] * blocks,
        out_shape=[jax.ShapeDtypeStruct((len(whole),) + block, jnp.float32)] * blocks,
        scratch_shapes=[
            pltpu.VMEM((len(whole), bin_count // SUB, windows, 2 * SUB), jnp.float32),
            pltpu.VMEM((blocks,) + block, jnp.float32),
        ],
        compiler_params=PARAMS,
    )(*in_vmem(held), *in_vmem([] if piece is None else [piece]), *in_vmem(before))


def partners(n, d):
    return [(i, i ^ d) for i in range(n)]


def after(value, *others):
    return lax.optimization_barrier((value,) + others)[0]


def shards(records, templates, masks, offsets):
    n_blk, n_chan, n_freq = (lax.axis_size(a) for a in ("blk", "chan", "freq"))
    windows, _, bin_count, _ = records.shape
    runs = bin_count // SUB
    blocks = n_chan * n_freq
    high, low = (jnp.asarray(t) for t in lag_tables())

    def exchange(found):
        return [found[0]] + [lax.ppermute(found[n], ("chan", "freq"), partners(blocks, n)) for n in range(1, blocks)]

    half = bin_count // 2
    mine = lax.dynamic_slice_in_dim(templates, lax.axis_index("parts") * half, half, 2)
    swap = lambda a: lax.ppermute(a, "parts", partners(2, 1))
    far = sorted(range(2, n_blk), key=lambda d: -(d & -d))
    final = far[-1]
    arrived = {far[0]: lax.ppermute(mine, "blk", partners(n_blk, far[0]))}
    near = lax.ppermute(templates, "blk", partners(n_blk, 1))
    held, spectra = own_template(masks, offsets, records, templates, high, low)
    for d in far[1:]:
        arrived[d] = lax.ppermute(after(mine, spectra), "blk", partners(n_blk, d))
    own, other = (0, runs // 2), (runs // 2, -(runs // 2))
    whole = {0: [(spectra, (0, 0))]}
    last = spectra
    for d in far[:-1]:
        swapped = swap(after(arrived[d], last))
        last = add_piece(held, d, own, arrived[d])
        whole[d] = [(last, own), (add_piece(held, d, other, after(swapped, last)), other)]
        last = whole[d][1][0]
    near = after(near, last)
    near_spectra = add_piece(held, 1, (0, 0), near)
    swapped = swap(after(arrived[final], near_spectra))
    late = add_piece(held, final, own, after(arrived[final], near_spectra))
    ready = list(whole)
    first = exchange(transform(held, [whole[d] for d in ready] + [[(after(near_spectra, late), (0, 0))]], blocks))
    second = exchange(finish(held, final, other, swapped, [[(late, own)]], blocks))
    return pl.pallas_call(
        functools.partial(sum_kernel, (ready + [1], [final])),
        in_specs=[IN_VMEM] * (2 * blocks),
        out_specs=IN_VMEM,
        out_shape=jax.ShapeDtypeStruct((n_blk, windows, NSAMP // blocks), jnp.float32),
        compiler_params=PARAMS,
    )(*first, *second)


def solution(mesh):
    placed = (P(("parts", "blk"), None, "freq", "chan"), P("blk", None, "freq", "chan"), P(), P())
    return jax.shard_map(
        shards,
        mesh=mesh,
        in_specs=placed,
        out_specs=P(None, ("parts", "blk"), ("chan", "freq")),
        check_vma=False,
    )
```

```python
import functools
import math

import jax
import jax.numpy as jnp
import numpy as np
from jax import lax
from jax.experimental import pallas as pl
from jax.experimental.pallas import tpu as pltpu
from jax.sharding import PartitionSpec as P

NSAMP = 1024
BINS = 512
SUB = 64
FOLD = 256
PIECES = 2
BATCH = 4
VMEM_LIMIT = 24 * 2**20


def lag_tables():
    bins = np.arange(BINS).reshape(-1, SUB)
    angle = 2.0 * math.pi / NSAMP * (bins[..., None] * np.arange(FOLD) % NSAMP)
    table = math.sqrt(2.0 / BINS) * np.concatenate([np.cos(angle), -np.sin(angle)], axis=1)
    table = table.astype(np.float32)
    high = table.astype(jnp.bfloat16)
    low = (table - high.astype(np.float32)).astype(jnp.bfloat16)
    return high, low


def two_halves(values):
    high = values.astype(jnp.bfloat16)
    return high, (values - high.astype(jnp.float32)).astype(jnp.bfloat16)


def product(left, right, contract):
    return lax.dot_general(left, right, ((contract[:1], contract[1:]), ((), ())), preferred_element_type=jnp.float32)


def mask_row(masks, template_at, width):
    here = masks.shape[1] // lax.axis_size("chan")
    first = lax.axis_index("chan") * here
    lane = lax.broadcasted_iota(jnp.int32, (1, width), 1) // (width // here)
    row = jnp.zeros((1, width), jnp.float32)
    for b in range(here):
        row = jnp.where(lane == b, masks[template_at, first + b].astype(jnp.float32), row)
    return row


def run_spectrum(template_at, run, piece, used, records, turn):
    windows, pairs = records.shape[0], records.shape[0] // 2
    bins = pl.ds(pl.multiple_of(run * SUB, SUB), SUB)
    mask = used[template_at].astype(jnp.bfloat16)
    first, second = piece[0] * mask, piece[1] * mask
    weights = jnp.concatenate(
        [jnp.concatenate([first, second], axis=1), jnp.concatenate([-second, first], axis=1)], axis=0
    )
    row = lax.broadcasted_iota(jnp.int32, (2 * SUB, 2 * SUB), 0)
    lane = lax.broadcasted_iota(jnp.int32, (2 * SUB, 2 * SUB), 1)
    same_bin = row % SUB == lane % SUB
    real, imag = [], []
    for v in range(pairs):
        rows = jnp.concatenate(
            [jnp.concatenate([records[w, 0, bins, :], records[w, 1, bins, :]], axis=1) for w in (v, v + pairs)], axis=0
        )
        every = jnp.where(same_bin, product(weights, rows, (1, 1)), 0.0)
        real.append(jnp.sum(every[:SUB], axis=0, keepdims=True))
        imag.append(jnp.sum(every[SUB:], axis=0, keepdims=True))
    real, imag = jnp.concatenate(real, axis=0), jnp.concatenate(imag, axis=0)
    real = jnp.concatenate([real, pltpu.roll(real, SUB, 1)], axis=0)
    imag = jnp.concatenate([pltpu.roll(imag, SUB, 1), imag], axis=0)
    real_lane = lax.broadcasted_iota(jnp.int32, (windows, 2 * SUB), 1) < SUB
    spectrum = jnp.where(real_lane, real, imag)
    cosine, sine_table = (turn[template_at, i, pl.ds(run, 1)] for i in range(2))
    return spectrum * cosine + pltpu.roll(spectrum, SUB, 1) * sine_table


def all_lags(spectra, high, low):
    runs, windows, width = spectra.shape
    real_lane = lax.broadcasted_iota(jnp.int32, (windows, width), 1) < SUB
    sign = jnp.where(real_lane, 1.0, -1.0)
    straight = jnp.concatenate([spectra[r] for r in range(runs)], axis=1)
    turned = jnp.concatenate([sign * pltpu.roll(spectra[r], SUB, 1) for r in range(runs)], axis=1)
    lane = lax.broadcasted_iota(jnp.int32, straight.shape, 1) % 4
    picked = [jnp.where(lane == r, straight, 0.0) for r in range(4)]
    picked += [jnp.where(lane == r, turned, 0.0) for r in (1, 3)]
    rows = jnp.concatenate(picked, axis=0)
    rows_high, rows_low = two_halves(rows)
    table_high, table_low = (jnp.concatenate([t[r] for r in range(runs)], axis=0) for t in (high, low))
    both = product(jnp.concatenate([rows_high, rows_low], axis=0), table_high, (1, 0))
    sums = both[: rows.shape[0]] + both[rows.shape[0] :] + product(rows_high, table_low, (1, 0))
    re0, re1, re2, re3, im1, im3 = (sums[i * windows : (i + 1) * windows] for i in range(6))
    even, odd, even_turned, odd_turned = re0 + re2, re1 + re3, re0 - re2, im1 - im3
    return [even + odd, even_turned - odd_turned, even - odd, even_turned + odd_turned]


def own_kernel(
    masks, offsets, records, templates, high, low, held, turn, used, held_high, held_low, spectra, theirs, template, numbers, sems
):
    runs = turn.shape[2]
    first_run = lax.axis_index("freq") * runs
    small = [
        pltpu.make_async_copy(masks, numbers[0], sems.at[0]),
        pltpu.make_async_copy(offsets, numbers[1], sems.at[1]),
    ]
    pieces = [
        pltpu.make_async_copy(values.at[:, :, pl.ds(r * SUB, SUB), :], to.at[:, :, pl.ds(r * SUB, SUB), :], sem)
        for r in range(runs)
        for values, to, sem in (
            (templates, template, sems.at[4 + 2 * r]),
            (records, held, sems.at[5 + 2 * r]),
        )
    ]
    tables = [
        pltpu.make_async_copy(table.at[pl.ds(first_run, runs)], to, sems.at[2 + i])
        for i, (table, to) in enumerate(((high, held_high), (low, held_low)))
    ]
    half = theirs.shape[2]
    from_bin = pl.multiple_of((1 - lax.axis_index("parts")) * half, half)
    tables.append(pltpu.make_async_copy(templates.at[:, :, pl.ds(from_bin, half), :], theirs, sems.at[4 + 2 * runs]))
    for copy in small + pieces + tables:
        copy.start()
    for copy in small:
        copy.wait()
    masks, offsets = numbers
    row = lax.broadcasted_iota(jnp.int32, (runs, 2 * SUB), 0)
    lane = lax.broadcasted_iota(jnp.int32, (runs, 2 * SUB), 1)
    bin_index = (first_run + row) * SUB + lane % SUB
    sign = jnp.where(lane < SUB, -1.0, 1.0)
    for t in range(turn.shape[0]):
        phase = offsets[t] * bin_index % NSAMP
        angle = 2.0 * math.pi / NSAMP * phase.astype(jnp.float32)
        turn[t, 0] = jnp.cos(angle)
        turn[t, 1] = jnp.sin(angle) * sign
        used[t] = mask_row(masks, t, held.shape[3])
    template_at = lax.axis_index("blk")
    for r in range(runs):
        for copy in pieces[2 * r : 2 * r + 2]:
            copy.wait()
        piece = template[0, :, r * SUB : (r + 1) * SUB, :]
        spectra[r] = run_spectrum(template_at, r, piece, used, held, turn)
    for copy in tables:
        copy.wait()


def piece_kernel(plan, held, turn, used, high, low, *rest):
    d, moved, whole = plan
    found = []
    if d is not None:
        piece, *rest = rest
        template_at = lax.axis_index("blk") ^ d
        first = lax.axis_index("parts") * moved[1] + moved[0]
        found = [
            run_spectrum(template_at, first + r, piece[0, :, r * SUB : (r + 1) * SUB, :], used, held, turn)
            for r in range(piece.shape[2] // SUB)
        ]
    if whole is None:
        for r, spectrum in enumerate(found):
            rest[0][r] = spectrum
        return
    n_in = sum(len(w) for w in whole)
    before, outs, (spectra, lags) = rest[:n_in], rest[n_in:-2], rest[-2:]
    at = 0
    for i, starts in enumerate(whole):
        for start, step in starts:
            run = lax.axis_index("parts") * step + start
            for r in range(before[at].shape[0]):
                spectra[i, run + r] = before[at][r]
            at += 1
    for r, spectrum in enumerate(found):
        spectra[len(whole) - 1, first + r] = spectrum
    me = lax.axis_index("chan") * lax.axis_size("freq") + lax.axis_index("freq")
    width = lags.shape[2]
    total = spectra.shape[0]
    for begin in range(0, total, BATCH):
        many = min(BATCH, total - begin)
        rows = jnp.concatenate([spectra[begin + i] for i in range(many)], axis=1)
        folded = all_lags(rows, high, low)
        for i in range(many):
            at = slice(i * held.shape[0], (i + 1) * held.shape[0])
            for n in range(len(outs)):
                start = n * width
                lags[n] = folded[start // FOLD][at, start % FOLD : start % FOLD + width]
            for n in range(len(outs)):
                outs[n][begin + i] = lags[me ^ n]


def sum_kernel(orders, *refs):
    *parts, out = refs
    per = len(parts) // len(orders)
    for g, order in enumerate(orders):
        for i, d in enumerate(order):
            total = parts[g * per][i]
            for part in parts[g * per + 1 : (g + 1) * per]:
                total += part[i]
            out[lax.axis_index("blk") ^ d] = total


IN_SMEM = pl.BlockSpec(memory_space=pltpu.SMEM)
IN_VMEM = pl.BlockSpec(memory_space=pltpu.VMEM)
IN_HBM = pl.BlockSpec(memory_space=pltpu.HBM)
PARAMS = pltpu.CompilerParams(vmem_limit_bytes=VMEM_LIMIT)


def in_vmem(values):
    return [pltpu.with_memory_space_constraint(v, pltpu.VMEM) for v in values]


def in_hbm(values):
    return [pltpu.with_memory_space_constraint(v, pltpu.HBM) for v in values]


def own_template(masks, offsets, records, template, high, low):
    windows, _, bin_count, width = records.shape
    runs = bin_count // SUB
    table = (runs,) + high.shape[1:]
    out_shape = [
        pltpu.VMEM(records.shape, records.dtype),
        pltpu.VMEM((offsets.shape[0], 2, runs, 2 * SUB), jnp.float32),
        pltpu.VMEM((offsets.shape[0], 1, width), jnp.float32),
        pltpu.VMEM(table, high.dtype),
        pltpu.VMEM(table, low.dtype),
        pltpu.VMEM((runs, windows, 2 * SUB), jnp.float32),
        pltpu.VMEM((1, 2, bin_count // 2, width), template.dtype),
    ]
    *held, spectra, theirs = pl.pallas_call(
        own_kernel,
        in_specs=[IN_HBM] * 6,
        out_specs=[IN_VMEM] * len(out_shape),
        out_shape=out_shape,
        scratch_shapes=[
            pltpu.VMEM(template.shape, template.dtype),
            (pltpu.SMEM(masks.shape, masks.dtype), pltpu.SMEM(offsets.shape, offsets.dtype)),
            pltpu.SemaphoreType.DMA((2 * runs + 5,)),
        ],
        compiler_params=PARAMS,
    )(*in_hbm((masks, offsets, records, template, high, low)))
    return held, spectra, theirs


def add_piece(held, d, moved, piece):
    windows = held[0].shape[0]
    return pl.pallas_call(
        functools.partial(piece_kernel, (d, moved, None)),
        in_specs=[IN_VMEM] * 6,
        out_specs=IN_VMEM,
        out_shape=pltpu.VMEM((piece.shape[2] // SUB, windows, 2 * SUB), jnp.float32),
        compiler_params=PARAMS,
    )(*in_vmem(held), *in_vmem([piece]))


def transform(held, whole, blocks):
    return finish(held, None, None, None, whole, blocks)


def finish(held, d, moved, piece, whole, blocks):
    windows, _, bin_count, _ = held[0].shape
    block = (windows, NSAMP // blocks)
    before = [spectra for pieces in whole for spectra, _ in pieces]
    places = tuple(tuple(at for _, at in pieces) for pieces in whole)
    return pl.pallas_call(
        functools.partial(piece_kernel, (d, moved, places)),
        in_specs=[IN_VMEM] * (len(held) + (piece is not None) + len(before)),
        out_specs=[IN_VMEM] * blocks,
        out_shape=[jax.ShapeDtypeStruct((len(whole),) + block, jnp.float32)] * blocks,
        scratch_shapes=[
            pltpu.VMEM((len(whole), bin_count // SUB, windows, 2 * SUB), jnp.float32),
            pltpu.VMEM((blocks,) + block, jnp.float32),
        ],
        compiler_params=PARAMS,
    )(*in_vmem(held), *in_vmem([] if piece is None else [piece]), *in_vmem(before))


def cut_kernel(template, *rest):
    *outs, sems = rest
    at = lax.axis_index("parts") * sum(out.shape[2] for out in outs)
    copies = []
    for i, out in enumerate(outs):
        bins = pl.ds(pl.multiple_of(at, SUB), out.shape[2])
        copies.append(pltpu.make_async_copy(template.at[:, :, bins, :], out, sems.at[i]))
        at += out.shape[2]
    for copy in copies:
        copy.start()
    for copy in copies:
        copy.wait()


def cut(template, count):
    shape = template.shape[:2] + (template.shape[2] // (2 * count),) + template.shape[3:]
    return pl.pallas_call(
        cut_kernel,
        in_specs=[IN_HBM],
        out_specs=[IN_VMEM] * count,
        out_shape=[pltpu.VMEM(shape, template.dtype)] * count,
        scratch_shapes=[pltpu.SemaphoreType.DMA((count,))],
        compiler_params=PARAMS,
    )(*in_hbm([template]))


def join_kernel(count, *refs):
    *pieces, out = refs
    width = pieces[0].shape[2]
    for i in range(count):
        out[:, :, i * width : (i + 1) * width, :] = pieces[i][...]
    if len(pieces) > count:

        @pl.when((lax.axis_index("blk") + 1) & 2 != 0)
        def _():
            out[...] = pieces[count][...]


def join(pieces, *middle):
    one = pieces[0]
    shape = one.shape[:2] + (len(pieces) * one.shape[2],) + one.shape[3:]
    operands = in_vmem([*pieces, *middle])
    return pl.pallas_call(
        functools.partial(join_kernel, len(pieces)),
        in_specs=[IN_VMEM] * len(operands),
        out_specs=IN_VMEM,
        out_shape=pltpu.VMEM(shape, one.dtype),
        compiler_params=PARAMS,
    )(*operands)


def partners(n, d):
    return [(i, i ^ d) for i in range(n)]


def after(value, *others):
    return lax.optimization_barrier((value,) + others)[0]


def swap(piece):
    return lax.ppermute(piece, "parts", partners(2, 1))


def any_line(held, spectra, templates, mine, exchange, transform_of, finish_of):
    n_blk, runs = lax.axis_size("blk"), held[0].shape[2] // SUB
    own, other = (0, runs // 2), (runs // 2, -(runs // 2))
    far = range(2, n_blk)
    whole = {0: [(spectra, (0, 0))]}
    last = spectra
    for d in far:
        arrived = lax.ppermute(after(mine, last), "blk", partners(n_blk, d))
        swapped = swap(arrived)
        last = add_piece(held, d, own, arrived)
        whole[d] = [(last, own), (add_piece(held, d, other, swapped), other)]
    near = lax.ppermute(templates, "blk", partners(n_blk, 1))
    order = list(whole)
    first = exchange(transform_of([whole[d] for d in order]))
    return (order, [1]), first + exchange(finish_of(1, (0, 0), near, [[]]))


def line_of_four(held, spectra, mine, theirs, arrived, near, exchange, transform_of, finish_of):
    runs = held[0].shape[2] // SUB
    own, other = (0, runs // 2), (runs // 2, -(runs // 2))
    arrived = [after(a, spectra) for a in arrived]
    middle = lax.ppermute(after(mine, spectra), "blk", [(0, 0), (1, 2), (2, 1), (3, 3)])
    ends = [lax.ppermute(a, "blk", partners(4, 1)) for a in arrived]
    arrived = join(arrived)
    swapped = swap(arrived)
    second = add_piece(held, 2, own, arrived)
    near_first = add_piece(held, 1, own, after(near, second))
    near = lax.ppermute(after(theirs, near_first), "blk", partners(4, 1))
    third = join(ends, middle)
    third_swapped = swap(third)
    third_first = add_piece(held, 3, own, third)
    second_rest = add_piece(held, 2, other, swapped)
    first = exchange(transform_of([[(spectra, (0, 0))], [(second, own), (second_rest, other)]]))
    near_rest = add_piece(held, 1, other, near)
    whole = [[(near_first, own), (near_rest, other)], [(third_first, own)]]
    return ([0, 2], [1, 3]), first + exchange(finish_of(3, other, third_swapped, whole))


def shards(records, templates, masks, offsets):
    n_blk, n_chan, n_freq = (lax.axis_size(a) for a in ("blk", "chan", "freq"))
    windows, _, bin_count, _ = records.shape
    blocks = n_chan * n_freq
    high, low = (jnp.asarray(t) for t in lag_tables())

    def exchange(found):
        return [found[0]] + [lax.ppermute(found[n], ("chan", "freq"), partners(blocks, n)) for n in range(1, blocks)]

    pieces = cut(templates, PIECES)
    if n_blk == 4:
        arrived = [lax.ppermute(piece, "blk", partners(n_blk, 2)) for piece in pieces]
        mine = join(pieces)
        near = lax.ppermute(mine, "blk", partners(n_blk, 1))
    held, spectra, theirs = own_template(masks, offsets, records, templates, high, low)
    after_all = (exchange, lambda whole: transform(held, whole, blocks), lambda *w: finish(held, *w, blocks))
    if n_blk == 4:
        orders, parts = line_of_four(held, spectra, mine, theirs, arrived, near, *after_all)
    else:
        orders, parts = any_line(held, spectra, templates, join(pieces), *after_all)
    return pl.pallas_call(
        functools.partial(sum_kernel, orders),
        in_specs=[IN_VMEM] * len(parts),
        out_specs=IN_VMEM,
        out_shape=jax.ShapeDtypeStruct((n_blk, windows, NSAMP // blocks), jnp.float32),
        compiler_params=PARAMS,
    )(*parts)


def solution(mesh):
    placed = (P(("parts", "blk"), None, "freq", "chan"), P("blk", None, "freq", "chan"), P(), P())
    return jax.shard_map(
        shards,
        mesh=mesh,
        in_specs=placed,
        out_specs=P(None, ("parts", "blk"), ("chan", "freq")),
        check_vma=False,
    )
```

```python
import functools
import math

import jax
import jax.numpy as jnp
import numpy as np
from jax import lax
from jax.experimental import pallas as pl
from jax.experimental.pallas import tpu as pltpu
from jax.sharding import PartitionSpec as P

NSAMP = 1024
BINS = 512
GROUP = 16
HALF = 128
RUN = 64
FOLD = 256
PIECES = 1
BATCH = 4
VMEM_LIMIT = 24 * 2**20


def lag_tables():
    bins = np.arange(BINS).reshape(-1, HALF)
    angle = 2.0 * math.pi / NSAMP * (bins[..., None] * np.arange(FOLD) % NSAMP)
    table = math.sqrt(2.0 / BINS) * np.concatenate([np.cos(angle), -np.sin(angle)], axis=1)
    table = table.astype(np.float32)
    high = table.astype(jnp.bfloat16)
    low = (table - high.astype(np.float32)).astype(jnp.bfloat16)
    return high, low


def two_halves(values):
    high = values.astype(jnp.bfloat16)
    return high, (values - high.astype(jnp.float32)).astype(jnp.bfloat16)


def product(left, right, contract):
    return lax.dot_general(left, right, ((contract[:1], contract[1:]), ((), ())), preferred_element_type=jnp.float32)


def mask_row(masks, template_at, width):
    here = masks.shape[1] // lax.axis_size("chan")
    first = lax.axis_index("chan") * here
    lane = lax.broadcasted_iota(jnp.int32, (1, width), 1) // (width // here)
    row = jnp.zeros((1, width), jnp.float32)
    for b in range(here):
        row = jnp.where(lane == b, masks[template_at, first + b].astype(jnp.float32), row)
    return row


def block_transpose(values):
    row = lax.broadcasted_iota(jnp.int32, values.shape, 0)
    place = lax.broadcasted_iota(jnp.int32, values.shape, 1) // GROUP
    for bit in (1, 2, 4):
        up = pltpu.roll(pltpu.roll(values, 8 - bit, 0), bit * GROUP, 1)
        down = pltpu.roll(pltpu.roll(values, bit, 0), 8 * GROUP - bit * GROUP, 1)
        moved = jnp.where(row & bit == 0, up, down)
        values = jnp.where(row & bit == place & bit, values, moved)
    return values


def group_rows(records, half, g):
    bins = pl.ds(pl.multiple_of(half * HALF + g * GROUP, GROUP), GROUP)
    return jnp.concatenate(
        [jnp.concatenate([records[w, 0, bins, :], records[w, 1, bins, :]], axis=1) for w in range(records.shape[0])],
        axis=0,
    )


def flip_kernel(records, out):
    for g in range(HALF // GROUP):
        out[g] = group_rows(records, 1 - lax.axis_index("parts"), g).T


def half_spectra(entries, half, records, turn, used, ready=None, flipped=None):
    windows = records.shape[0]
    masks = [used[template_at].astype(jnp.bfloat16) for template_at, _ in entries]
    row = lax.broadcasted_iota(jnp.int32, (2 * GROUP * len(entries), windows * GROUP), 0)
    lane = lax.broadcasted_iota(jnp.int32, (2 * GROUP * len(entries), windows * GROUP), 1)
    same_bin = row % GROUP == lane % GROUP
    sums = [[] for _ in range(2 * len(entries))]
    for g in range(HALF // GROUP):
        if ready is not None:
            ready(g)
        weights = []
        for (_, pieces), mask in zip(entries, masks):
            piece = pieces[g * GROUP // pieces[0].shape[2]]
            start = g * GROUP % piece.shape[2]
            first, second = (piece[0, part, start : start + GROUP, :] * mask for part in range(2))
            weights.append(jnp.concatenate([first, second], axis=1))
            weights.append(jnp.concatenate([-second, first], axis=1))
        weights = jnp.concatenate(weights, axis=0)
        if flipped is None:
            every = product(weights, group_rows(records, half, g), (1, 1))
        else:
            every = product(weights, flipped[g], (1, 0))
        every = jnp.where(same_bin, every, 0.0)
        for i, found in enumerate(sums):
            found.append(jnp.sum(every[i * GROUP : (i + 1) * GROUP], axis=0, keepdims=True))
    wide = 8 * GROUP
    turned = []
    for i, (template_at, _) in enumerate(entries):
        real, imag = (
            jnp.concatenate(
                [block_transpose(found[:, at : at + wide]) for at in range(0, windows * GROUP, wide)], axis=0
            )
            for found in (jnp.concatenate(sums[2 * i + part], axis=0) for part in range(2))
        )
        cosine, sine_table = (turn[template_at, part, pl.ds(half, 1)] for part in range(2))
        turned.append((real * cosine - imag * sine_table, real * sine_table + imag * cosine))
    return turned


def all_lags(parts, high, low):
    windows = parts[0][0].shape[0]
    straight = jnp.concatenate([v for real, imag in parts for v in (real, imag)], axis=1)
    turned = jnp.concatenate([v for real, imag in parts for v in (imag, -real)], axis=1)
    lane = lax.broadcasted_iota(jnp.int32, straight.shape, 1) % 4
    picked = [jnp.where(lane == r, straight, 0.0) for r in range(4)]
    picked += [jnp.where(lane == r, turned, 0.0) for r in (1, 3)]
    rows = jnp.concatenate(picked, axis=0)
    rows_high, rows_low = two_halves(rows)
    table_high, table_low = (jnp.concatenate([t[r] for r in range(len(parts))], axis=0) for t in (high, low))
    both = product(jnp.concatenate([rows_high, rows_low], axis=0), table_high, (1, 0))
    sums = both[: rows.shape[0]] + both[rows.shape[0] :] + product(rows_high, table_low, (1, 0))
    re0, re1, re2, re3, im1, im3 = (sums[i * windows : (i + 1) * windows] for i in range(6))
    even, odd, even_turned, odd_turned = re0 + re2, re1 + re3, re0 - re2, im1 - im3
    return [even + odd, even_turned - odd_turned, even - odd, even_turned + odd_turned]


def own_kernel(
    masks, offsets, records, templates, high, low, held, turn, used, held_high, held_low, spectra, theirs, rest, template, numbers, sems
):
    halves = turn.shape[2]
    runs = records.shape[2] // RUN
    first_half = lax.axis_index("freq") * halves
    small = [
        pltpu.make_async_copy(masks, numbers[0], sems.at[0]),
        pltpu.make_async_copy(offsets, numbers[1], sems.at[1]),
    ]
    pieces = [
        pltpu.make_async_copy(values.at[:, :, pl.ds(r * RUN, RUN), :], to.at[:, :, pl.ds(r * RUN, RUN), :], sem)
        for r in range(runs)
        for values, to, sem in (
            (templates, template, sems.at[5 + 2 * r]),
            (records, held, sems.at[6 + 2 * r]),
        )
        if r < HALF // RUN or to is held
    ]
    tables = [
        pltpu.make_async_copy(table.at[pl.ds(first_half, halves)], to, sems.at[2 + i])
        for i, (table, to) in enumerate(((high, held_high), (low, held_low)))
    ]
    from_bin = pl.multiple_of((1 - lax.axis_index("parts")) * HALF, HALF)
    tables.append(pltpu.make_async_copy(templates.at[:, :, pl.ds(from_bin, HALF), :], theirs, sems.at[4]))
    tables.append(pltpu.make_async_copy(templates.at[:, :, pl.ds(HALF, rest.shape[2]), :], rest, sems.at[5 + 2 * runs]))
    for copy in small + pieces + tables:
        copy.start()
    for copy in small:
        copy.wait()
    masks, offsets = numbers
    row = lax.broadcasted_iota(jnp.int32, (halves, HALF), 0)
    lane = lax.broadcasted_iota(jnp.int32, (halves, HALF), 1)
    bin_index = (first_half + row) * HALF + lane
    for t in range(turn.shape[0]):
        phase = offsets[t] * bin_index % NSAMP
        angle = 2.0 * math.pi / NSAMP * phase.astype(jnp.float32)
        turn[t, 0] = jnp.cos(angle)
        turn[t, 1] = jnp.sin(angle)
        used[t] = mask_row(masks, t, held.shape[3])
    template_at = lax.axis_index("blk")

    def ready(g):
        if g * GROUP % RUN == 0:
            at = 2 * g * GROUP // RUN
            for copy in pieces[at : at + 2]:
                copy.wait()

    ((spectra[0], spectra[1]),) = half_spectra([(template_at, [template])], 0, held, turn, used, ready)
    for copy in pieces[2 * HALF // RUN :] + tables:
        copy.wait()


def pieces_kernel(plan, held, turn, used, *refs):
    ds, counts, own = plan
    *refs, out = refs
    entries = []
    for d, count in zip(ds, counts):
        entries.append((lax.axis_index("blk") ^ d, refs[:count]))
        refs = refs[count:]
    found = half_spectra(entries, lax.axis_index("parts") if own else 1, held, turn, used)
    for i, (real, imag) in enumerate(found):
        out[i, 0] = real
        out[i, 1] = imag


def lags_kernel(plan, held, turn, used, high, low, flipped, *refs):
    ds, counts, n_whole = plan
    *refs, spectra, lags = refs
    outs = refs[-lags.shape[0] :]
    whole, early, refs = refs[: 2 * n_whole], refs[2 * n_whole], refs[2 * n_whole + 1 : -lags.shape[0]]
    part = lax.axis_index("parts")
    entries = []
    for d, count in zip(ds, counts):
        entries.append((lax.axis_index("blk") ^ d, refs[:count]))
        refs = refs[count:]
    for i in range(n_whole):
        spectra[i, 0] = whole[2 * i][...]
        spectra[i, 1] = whole[2 * i + 1][0]
    found = half_spectra(entries, 1 - part, held, turn, used, flipped=flipped)
    for i, (real, imag) in enumerate(found):
        spectra[n_whole + i, part] = early[i]
        spectra[n_whole + i, 1 - part, 0] = real
        spectra[n_whole + i, 1 - part, 1] = imag
    me = lax.axis_index("chan") * lax.axis_size("freq") + lax.axis_index("freq")
    blocks, windows, width = lags.shape
    total, halves = spectra.shape[:2]
    parts = [
        tuple(jnp.concatenate([spectra[i, h, part] for i in range(total)], axis=0) for part in range(2))
        for h in range(halves)
    ]
    folded = all_lags(parts, high, low)
    for i in range(total):
        at = slice(i * windows, (i + 1) * windows)
        for n in range(blocks):
            start = n * width
            lags[n] = folded[start // FOLD][at, start % FOLD : start % FOLD + width]
        for n in range(blocks):
            outs[n][i] = lags[me ^ n]


def sum_kernel(orders, *refs):
    *parts, out = refs
    per = len(parts) // len(orders)
    for g, order in enumerate(orders):
        for i, d in enumerate(order):
            total = parts[g * per][i]
            for part in parts[g * per + 1 : (g + 1) * per]:
                total += part[i]
            out[lax.axis_index("blk") ^ d] = total


IN_VMEM = pl.BlockSpec(memory_space=pltpu.VMEM)
IN_HBM = pl.BlockSpec(memory_space=pltpu.HBM)
PARAMS = pltpu.CompilerParams(vmem_limit_bytes=VMEM_LIMIT)


def in_vmem(values):
    return [pltpu.with_memory_space_constraint(v, pltpu.VMEM) for v in values]


def in_hbm(values):
    return [pltpu.with_memory_space_constraint(v, pltpu.HBM) for v in values]


def own_template(masks, offsets, records, template, high, low):
    windows, _, bin_count, width = records.shape
    halves = bin_count // HALF
    table = (halves,) + high.shape[1:]
    out_shape = [
        pltpu.VMEM(records.shape, records.dtype),
        pltpu.VMEM((offsets.shape[0], 2, halves, HALF), jnp.float32),
        pltpu.VMEM((offsets.shape[0], 1, width), jnp.float32),
        pltpu.VMEM(table, high.dtype),
        pltpu.VMEM(table, low.dtype),
        pltpu.VMEM((2, windows, HALF), jnp.float32),
        pltpu.VMEM((1, 2, HALF, width), template.dtype),
        pltpu.VMEM((1, 2, bin_count - HALF, width), template.dtype),
    ]
    *held, spectra, theirs, rest = pl.pallas_call(
        own_kernel,
        in_specs=[IN_HBM] * 6,
        out_specs=[IN_VMEM] * len(out_shape),
        out_shape=out_shape,
        scratch_shapes=[
            pltpu.VMEM((1, 2, HALF, width), template.dtype),
            (pltpu.SMEM(masks.shape, masks.dtype), pltpu.SMEM(offsets.shape, offsets.dtype)),
            pltpu.SemaphoreType.DMA((2 * (bin_count // RUN) + 6,)),
        ],
        compiler_params=PARAMS,
    )(*in_hbm((masks, offsets, records, template, high, low)))
    return held, spectra, theirs, rest


def early_half(held, entries, own=True):
    windows = held[0].shape[0]
    plan = (tuple(d for d, _ in entries), tuple(len(pieces) for _, pieces in entries), own)
    operands = in_vmem([*held[:3], *(piece for _, pieces in entries for piece in pieces)])
    return pl.pallas_call(
        functools.partial(pieces_kernel, plan),
        in_specs=[IN_VMEM] * len(operands),
        out_specs=IN_VMEM,
        out_shape=pltpu.VMEM((len(entries), 2, windows, HALF), jnp.float32),
        compiler_params=PARAMS,
    )(*operands)


def flip(held):
    windows, _, _, width = held[0].shape
    return pl.pallas_call(
        flip_kernel,
        in_specs=[IN_VMEM],
        out_specs=IN_VMEM,
        out_shape=pltpu.VMEM((HALF // GROUP, 2 * width, windows * GROUP), held[0].dtype),
        compiler_params=PARAMS,
    )(*in_vmem(held[:1]))


def lag_blocks(held, flipped, early, entries, whole, blocks):
    windows = held[0].shape[0]
    halves = held[0].shape[2] // HALF
    count = len(whole) + len(entries)
    block = (windows, NSAMP // blocks)
    plan = (tuple(d for d, _ in entries), tuple(len(pieces) for _, pieces in entries), len(whole))
    operands = in_vmem([*held, flipped, *(half for pair in whole for half in pair), early, *(piece for _, pieces in entries for piece in pieces)])
    return pl.pallas_call(
        functools.partial(lags_kernel, plan),
        in_specs=[IN_VMEM] * len(operands),
        out_specs=[IN_VMEM] * blocks,
        out_shape=[jax.ShapeDtypeStruct((count,) + block, jnp.float32)] * blocks,
        scratch_shapes=[
            pltpu.VMEM((count, halves, 2, windows, HALF), jnp.float32),
            pltpu.VMEM((blocks,) + block, jnp.float32),
        ],
        compiler_params=PARAMS,
    )(*operands)


def cut_kernel(template, *rest):
    *outs, sems = rest
    at = lax.axis_index("parts") * sum(out.shape[2] for out in outs)
    copies = []
    for i, out in enumerate(outs):
        bins = pl.ds(pl.multiple_of(at, GROUP), out.shape[2])
        copies.append(pltpu.make_async_copy(template.at[:, :, bins, :], out, sems.at[i]))
        at += out.shape[2]
    for copy in copies:
        copy.start()
    for copy in copies:
        copy.wait()


def cut(template, count):
    shape = template.shape[:2] + (template.shape[2] // (2 * count),) + template.shape[3:]
    return pl.pallas_call(
        cut_kernel,
        in_specs=[IN_HBM],
        out_specs=[IN_VMEM] * count,
        out_shape=[pltpu.VMEM(shape, template.dtype)] * count,
        scratch_shapes=[pltpu.SemaphoreType.DMA((count,))],
        compiler_params=PARAMS,
    )(*in_hbm([template]))


def join_kernel(count, *refs):
    *pieces, out = refs
    width = pieces[0].shape[2]
    for i in range(count):
        out[:, :, i * width : (i + 1) * width, :] = pieces[i][...]
    if len(pieces) > count:

        @pl.when((lax.axis_index("blk") + 1) & 2 != 0)
        def _():
            out[...] = pieces[count][...]


def join(pieces, *middle):
    one = pieces[0]
    shape = one.shape[:2] + (len(pieces) * one.shape[2],) + one.shape[3:]
    operands = in_vmem([*pieces, *middle])
    return pl.pallas_call(
        functools.partial(join_kernel, len(pieces)),
        in_specs=[IN_VMEM] * len(operands),
        out_specs=IN_VMEM,
        out_shape=pltpu.VMEM(shape, one.dtype),
        compiler_params=PARAMS,
    )(*operands)


def partners(n, d):
    return [(i, i ^ d) for i in range(n)]


def after(value, *others):
    return lax.optimization_barrier((value,) + others)[0]


def swap(piece):
    return lax.ppermute(piece, "parts", partners(2, 1))


def any_line(held, mine, own, exchange, lags_of):
    n_blk = lax.axis_size("blk")
    orders, parts = [], []
    for begin in range(1, n_blk, BATCH):
        order = range(begin, min(begin + BATCH, n_blk))
        arrived = [lax.ppermute(mine, "blk", partners(n_blk, d)) for d in order]
        early = early_half(held, [(d, [a]) for d, a in zip(order, arrived)])
        whole = [own] if begin == 1 else []
        parts += exchange(lags_of(early, [(d, [swap(a)]) for d, a in zip(order, arrived)], whole))
        orders.append((0,) * len(whole) + tuple(order))
    return orders, parts


def line_of_four(held, mine, theirs, arrived, near, rest, spectra, flipped, exchange, lags_of):
    own = (spectra, early_half(held, [(0, [rest])], False))
    middle = lax.ppermute(after(mine, spectra), "blk", [(0, 0), (1, 2), (2, 1), (3, 3)])
    arrived = [after(a, own[1], flipped) for a in arrived]
    ends = [lax.ppermute(a, "blk", partners(4, 1)) for a in arrived]
    swapped = swap(join([after(arrived[0], near), *arrived[1:]]))
    third = join(ends, middle)
    third_swapped = swap(third)
    near_rest = lax.ppermute(after(theirs, third), "blk", partners(4, 1))
    early = early_half(held, [(1, [near]), (2, arrived), (3, [third])])
    parts = exchange(lags_of(early, [(1, [near_rest]), (2, [swapped]), (3, [third_swapped])], [own]))
    return [(0, 1, 2, 3)], parts


def shards(records, templates, masks, offsets):
    n_blk, n_chan, n_freq = (lax.axis_size(a) for a in ("blk", "chan", "freq"))
    windows = records.shape[0]
    blocks = n_chan * n_freq
    high, low = (jnp.asarray(t) for t in lag_tables())

    def exchange(found):
        return [found[0]] + [lax.ppermute(found[n], ("chan", "freq"), partners(blocks, n)) for n in range(1, blocks)]

    pieces = cut(templates, PIECES)
    mine = join(pieces)
    if n_blk == 4:
        arrived = [lax.ppermute(piece, "blk", partners(n_blk, 2)) for piece in pieces]
        near = lax.ppermute(mine, "blk", partners(n_blk, 1))
    held, spectra, theirs, rest = own_template(masks, offsets, records, templates, high, low)
    flipped = flip(held)
    after_all = (exchange, lambda *found: lag_blocks(held, flipped, *found, blocks))
    if n_blk == 4:
        orders, parts = line_of_four(held, mine, theirs, arrived, near, rest, spectra, flipped, *after_all)
    else:
        own = (spectra, early_half(held, [(0, [rest])], False))
        orders, parts = any_line(held, mine, own, *after_all)
    return pl.pallas_call(
        functools.partial(sum_kernel, orders),
        in_specs=[IN_VMEM] * len(parts),
        out_specs=IN_VMEM,
        out_shape=jax.ShapeDtypeStruct((n_blk, windows, NSAMP // blocks), jnp.float32),
        compiler_params=PARAMS,
    )(*parts)


def solution(mesh):
    placed = (P(("parts", "blk"), None, "freq", "chan"), P("blk", None, "freq", "chan"), P(), P())
    return jax.shard_map(
        shards,
        mesh=mesh,
        in_specs=placed,
        out_specs=P(None, ("parts", "blk"), ("chan", "freq")),
        check_vma=False,
    )
```

```python
import functools
import math

import jax
import jax.numpy as jnp
import numpy as np
from jax import lax
from jax.experimental import pallas as pl
from jax.experimental.pallas import tpu as pltpu
from jax.sharding import PartitionSpec as P

NSAMP = 1024
BINS = 512
GROUP = 16
HALF = 128
RUN = 64
FOLD = 256
PIECES = 1
BATCH = 4
OWN, OTHER = 2, 3
VMEM_LIMIT = 24 * 2**20


def lag_tables():
    bins = np.arange(BINS).reshape(-1, HALF)
    angle = 2.0 * math.pi / NSAMP * (bins[..., None] * np.arange(FOLD) % NSAMP)
    table = math.sqrt(2.0 / BINS) * np.concatenate([np.cos(angle), -np.sin(angle)], axis=1)
    table = table.astype(np.float32)
    high = table.astype(jnp.bfloat16)
    low = (table - high.astype(np.float32)).astype(jnp.bfloat16)
    return high, low


def two_halves(values):
    high = values.astype(jnp.bfloat16)
    return high, (values - high.astype(jnp.float32)).astype(jnp.bfloat16)


def product(left, right, contract):
    return lax.dot_general(left, right, ((contract[:1], contract[1:]), ((), ())), preferred_element_type=jnp.float32)


def mask_row(masks, template_at, width):
    here = masks.shape[1] // lax.axis_size("chan")
    first = lax.axis_index("chan") * here
    lane = lax.broadcasted_iota(jnp.int32, (1, width), 1) // (width // here)
    row = jnp.zeros((1, width), jnp.float32)
    for b in range(here):
        row = jnp.where(lane == b, masks[template_at, first + b].astype(jnp.float32), row)
    return row


def block_transpose(values):
    row = lax.broadcasted_iota(jnp.int32, values.shape, 0)
    place = lax.broadcasted_iota(jnp.int32, values.shape, 1) // GROUP
    for bit in (1, 2, 4):
        up = pltpu.roll(pltpu.roll(values, 8 - bit, 0), bit * GROUP, 1)
        down = pltpu.roll(pltpu.roll(values, bit, 0), 8 * GROUP - bit * GROUP, 1)
        moved = jnp.where(row & bit == 0, up, down)
        values = jnp.where(row & bit == place & bit, values, moved)
    return values


def group_rows(records, half, g):
    bins = pl.ds(pl.multiple_of(half * HALF + g * GROUP, GROUP), GROUP)
    return jnp.concatenate(
        [jnp.concatenate([records[w, 0, bins, :], records[w, 1, bins, :]], axis=1) for w in range(records.shape[0])],
        axis=0,
    )


def flip_kernel(records, out):
    for g in range(HALF // GROUP):
        out[g] = group_rows(records, 1 - lax.axis_index("parts"), g).T


def half_spectra(entries, half, records, turn, used, ready=None, flipped=None):
    windows = records.shape[0]
    masks = [used[template_at].astype(jnp.bfloat16) for template_at, _ in entries]
    row = lax.broadcasted_iota(jnp.int32, (2 * GROUP * len(entries), windows * GROUP), 0)
    lane = lax.broadcasted_iota(jnp.int32, (2 * GROUP * len(entries), windows * GROUP), 1)
    same_bin = row % GROUP == lane % GROUP
    sums = [[] for _ in range(2 * len(entries))]
    for g in range(HALF // GROUP):
        if ready is not None:
            ready(g)
        weights = []
        for (_, pieces), mask in zip(entries, masks):
            piece = pieces[g * GROUP // pieces[0].shape[2]]
            start = g * GROUP % piece.shape[2]
            first, second = (piece[0, part, start : start + GROUP, :] * mask for part in range(2))
            weights.append(jnp.concatenate([first, second], axis=1))
            weights.append(jnp.concatenate([-second, first], axis=1))
        weights = jnp.concatenate(weights, axis=0)
        if flipped is None:
            every = product(weights, group_rows(records, half, g), (1, 1))
        else:
            every = product(weights, flipped[g], (1, 0))
        every = jnp.where(same_bin, every, 0.0)
        for i, found in enumerate(sums):
            found.append(jnp.sum(every[i * GROUP : (i + 1) * GROUP], axis=0, keepdims=True))
    wide = 8 * GROUP
    turned = []
    for i, (template_at, _) in enumerate(entries):
        real, imag = (
            jnp.concatenate(
                [block_transpose(found[:, at : at + wide]) for at in range(0, windows * GROUP, wide)], axis=0
            )
            for found in (jnp.concatenate(sums[2 * i + part], axis=0) for part in range(2))
        )
        cosine, sine_table = (turn[template_at, part, pl.ds(half, 1)] for part in range(2))
        turned.append((real * cosine - imag * sine_table, real * sine_table + imag * cosine))
    return turned


def all_lags(parts, high, low):
    windows = parts[0][0].shape[0]
    straight = jnp.concatenate([v for real, imag in parts for v in (real, imag)], axis=1)
    turned = jnp.concatenate([v for real, imag in parts for v in (imag, -real)], axis=1)
    lane = lax.broadcasted_iota(jnp.int32, straight.shape, 1) % 4
    picked = [jnp.where(lane == r, straight, 0.0) for r in range(4)]
    picked += [jnp.where(lane == r, turned, 0.0) for r in (1, 3)]
    rows = jnp.concatenate(picked, axis=0)
    rows_high, rows_low = two_halves(rows)
    table_high, table_low = (jnp.concatenate([t[r] for r in range(len(parts))], axis=0) for t in (high, low))
    both = product(jnp.concatenate([rows_high, rows_low], axis=0), table_high, (1, 0))
    sums = both[: rows.shape[0]] + both[rows.shape[0] :] + product(rows_high, table_low, (1, 0))
    re0, re1, re2, re3, im1, im3 = (sums[i * windows : (i + 1) * windows] for i in range(6))
    even, odd, even_turned, odd_turned = re0 + re2, re1 + re3, re0 - re2, im1 - im3
    return [even + odd, even_turned - odd_turned, even - odd, even_turned + odd_turned]


def own_kernel(
    masks, offsets, records, templates, high, low, held, turn, used, held_high, held_low, spectra, theirs, rest, template, numbers, sems
):
    halves = turn.shape[2]
    runs = records.shape[2] // RUN
    first_half = lax.axis_index("freq") * halves
    small = [
        pltpu.make_async_copy(masks, numbers[0], sems.at[0]),
        pltpu.make_async_copy(offsets, numbers[1], sems.at[1]),
    ]
    pieces = [
        pltpu.make_async_copy(values.at[:, :, pl.ds(r * RUN, RUN), :], to.at[:, :, pl.ds(r * RUN, RUN), :], sem)
        for r in range(runs)
        for values, to, sem in (
            (templates, template, sems.at[5 + 2 * r]),
            (records, held, sems.at[6 + 2 * r]),
        )
        if r < HALF // RUN or to is held
    ]
    tables = [
        pltpu.make_async_copy(table.at[pl.ds(first_half, halves)], to, sems.at[2 + i])
        for i, (table, to) in enumerate(((high, held_high), (low, held_low)))
    ]
    from_bin = pl.multiple_of((1 - lax.axis_index("parts")) * HALF, HALF)
    tables.append(pltpu.make_async_copy(templates.at[:, :, pl.ds(from_bin, HALF), :], theirs, sems.at[4]))
    tables.append(pltpu.make_async_copy(templates.at[:, :, pl.ds(HALF, rest.shape[2]), :], rest, sems.at[5 + 2 * runs]))
    for copy in small + pieces + tables:
        copy.start()
    for copy in small:
        copy.wait()
    masks, offsets = numbers
    row = lax.broadcasted_iota(jnp.int32, (halves, HALF), 0)
    lane = lax.broadcasted_iota(jnp.int32, (halves, HALF), 1)
    bin_index = (first_half + row) * HALF + lane
    for t in range(turn.shape[0]):
        phase = offsets[t] * bin_index % NSAMP
        angle = 2.0 * math.pi / NSAMP * phase.astype(jnp.float32)
        turn[t, 0] = jnp.cos(angle)
        turn[t, 1] = jnp.sin(angle)
        used[t] = mask_row(masks, t, held.shape[3])
    template_at = lax.axis_index("blk")

    def ready(g):
        if g * GROUP % RUN == 0:
            at = 2 * g * GROUP // RUN
            for copy in pieces[at : at + 2]:
                copy.wait()

    ((spectra[0, 0], spectra[0, 1]),) = half_spectra([(template_at, [template])], 0, held, turn, used, ready)
    for copy in pieces[2 * HALF // RUN :] + tables:
        copy.wait()


def half_at(place):
    part = lax.axis_index("parts")
    return {OWN: part, OTHER: 1 - part}.get(place, place)


def entries_of(ds, counts, refs):
    entries = []
    for d, count in zip(ds, counts):
        entries.append((lax.axis_index("blk") ^ d, refs[:count]))
        refs = refs[count:]
    return entries


def pieces_kernel(plan, held, turn, used, *refs):
    ds, counts, place = plan
    *refs, out = refs
    found = half_spectra(entries_of(ds, counts, refs), half_at(place), held, turn, used)
    for i, (real, imag) in enumerate(found):
        out[i, 0] = real
        out[i, 1] = imag


def lags_kernel(plan, held, turn, used, high, low, flipped, *refs):
    ds, counts, known = plan
    *refs, spectra, lags = refs
    outs = refs[-lags.shape[0] :]
    for ref, (first, place) in zip(refs, known):
        for i in range(ref.shape[0]):
            spectra[first + i, half_at(place)] = ref[i]
    entries = entries_of(ds, counts, refs[len(known) : -lags.shape[0]])
    found = half_spectra(entries, half_at(OTHER), held, turn, used, flipped=flipped)
    for i, (real, imag) in enumerate(found):
        at = spectra.shape[0] - len(entries) + i
        spectra[at, half_at(OTHER), 0] = real
        spectra[at, half_at(OTHER), 1] = imag
    me = lax.axis_index("chan") * lax.axis_size("freq") + lax.axis_index("freq")
    blocks, windows, width = lags.shape
    total, halves = spectra.shape[:2]
    parts = [
        tuple(jnp.concatenate([spectra[i, h, part] for i in range(total)], axis=0) for part in range(2))
        for h in range(halves)
    ]
    folded = all_lags(parts, high, low)
    for i in range(total):
        at = slice(i * windows, (i + 1) * windows)
        for n in range(blocks):
            start = n * width
            lags[n] = folded[start // FOLD][at, start % FOLD : start % FOLD + width]
        for n in range(blocks):
            outs[n][i] = lags[me ^ n]


def sum_kernel(orders, *refs):
    *parts, out = refs
    per = len(parts) // len(orders)
    for g, order in enumerate(orders):
        for i, d in enumerate(order):
            total = parts[g * per][i]
            for part in parts[g * per + 1 : (g + 1) * per]:
                total += part[i]
            out[lax.axis_index("blk") ^ d] = total


IN_VMEM = pl.BlockSpec(memory_space=pltpu.VMEM)
IN_HBM = pl.BlockSpec(memory_space=pltpu.HBM)
PARAMS = pltpu.CompilerParams(vmem_limit_bytes=VMEM_LIMIT)


def in_vmem(values):
    return [pltpu.with_memory_space_constraint(v, pltpu.VMEM) for v in values]


def in_hbm(values):
    return [pltpu.with_memory_space_constraint(v, pltpu.HBM) for v in values]


def own_template(masks, offsets, records, template, high, low):
    windows, _, bin_count, width = records.shape
    halves = bin_count // HALF
    table = (halves,) + high.shape[1:]
    out_shape = [
        pltpu.VMEM(records.shape, records.dtype),
        pltpu.VMEM((offsets.shape[0], 2, halves, HALF), jnp.float32),
        pltpu.VMEM((offsets.shape[0], 1, width), jnp.float32),
        pltpu.VMEM(table, high.dtype),
        pltpu.VMEM(table, low.dtype),
        pltpu.VMEM((1, 2, windows, HALF), jnp.float32),
        pltpu.VMEM((1, 2, HALF, width), template.dtype),
        pltpu.VMEM((1, 2, bin_count - HALF, width), template.dtype),
    ]
    *held, spectra, theirs, rest = pl.pallas_call(
        own_kernel,
        in_specs=[IN_HBM] * 6,
        out_specs=[IN_VMEM] * len(out_shape),
        out_shape=out_shape,
        scratch_shapes=[
            pltpu.VMEM((1, 2, HALF, width), template.dtype),
            (pltpu.SMEM(masks.shape, masks.dtype), pltpu.SMEM(offsets.shape, offsets.dtype)),
            pltpu.SemaphoreType.DMA((2 * (bin_count // RUN) + 6,)),
        ],
        compiler_params=PARAMS,
    )(*in_hbm((masks, offsets, records, template, high, low)))
    return held, spectra, theirs, rest


def early_half(held, entries, place):
    windows = held[0].shape[0]
    plan = (tuple(d for d, _ in entries), tuple(len(pieces) for _, pieces in entries), place)
    operands = in_vmem([*held[:3], *(piece for _, pieces in entries for piece in pieces)])
    return pl.pallas_call(
        functools.partial(pieces_kernel, plan),
        in_specs=[IN_VMEM] * len(operands),
        out_specs=IN_VMEM,
        out_shape=pltpu.VMEM((len(entries), 2, windows, HALF), jnp.float32),
        compiler_params=PARAMS,
    )(*operands)


def flip(held):
    windows, _, _, width = held[0].shape
    return pl.pallas_call(
        flip_kernel,
        in_specs=[IN_VMEM],
        out_specs=IN_VMEM,
        out_shape=pltpu.VMEM((HALF // GROUP, 2 * width, windows * GROUP), held[0].dtype),
        compiler_params=PARAMS,
    )(*in_vmem(held[:1]))


def lag_blocks(held, flipped, known, entries, count, blocks):
    windows = held[0].shape[0]
    halves = held[0].shape[2] // HALF
    block = (windows, NSAMP // blocks)
    plan = (
        tuple(d for d, _ in entries),
        tuple(len(pieces) for _, pieces in entries),
        tuple((first, place) for _, first, place in known),
    )
    operands = in_vmem([*held, flipped, *(k[0] for k in known), *(piece for _, pieces in entries for piece in pieces)])
    return pl.pallas_call(
        functools.partial(lags_kernel, plan),
        in_specs=[IN_VMEM] * len(operands),
        out_specs=[IN_VMEM] * blocks,
        out_shape=[jax.ShapeDtypeStruct((count,) + block, jnp.float32)] * blocks,
        scratch_shapes=[
            pltpu.VMEM((count, halves, 2, windows, HALF), jnp.float32),
            pltpu.VMEM((blocks,) + block, jnp.float32),
        ],
        compiler_params=PARAMS,
    )(*operands)


def cut_kernel(template, *rest):
    *outs, sems = rest
    at = lax.axis_index("parts") * sum(out.shape[2] for out in outs)
    copies = []
    for i, out in enumerate(outs):
        bins = pl.ds(pl.multiple_of(at, GROUP), out.shape[2])
        copies.append(pltpu.make_async_copy(template.at[:, :, bins, :], out, sems.at[i]))
        at += out.shape[2]
    for copy in copies:
        copy.start()
    for copy in copies:
        copy.wait()


def cut(template, count):
    shape = template.shape[:2] + (template.shape[2] // (2 * count),) + template.shape[3:]
    return pl.pallas_call(
        cut_kernel,
        in_specs=[IN_HBM],
        out_specs=[IN_VMEM] * count,
        out_shape=[pltpu.VMEM(shape, template.dtype)] * count,
        scratch_shapes=[pltpu.SemaphoreType.DMA((count,))],
        compiler_params=PARAMS,
    )(*in_hbm([template]))


def join_kernel(count, *refs):
    *pieces, out = refs
    width = pieces[0].shape[2]
    for i in range(count):
        out[:, :, i * width : (i + 1) * width, :] = pieces[i][...]
    if len(pieces) > count:

        @pl.when((lax.axis_index("blk") + 1) & 2 != 0)
        def _():
            out[...] = pieces[count][...]


def join(pieces, *middle):
    one = pieces[0]
    shape = one.shape[:2] + (len(pieces) * one.shape[2],) + one.shape[3:]
    operands = in_vmem([*pieces, *middle])
    return pl.pallas_call(
        functools.partial(join_kernel, len(pieces)),
        in_specs=[IN_VMEM] * len(operands),
        out_specs=IN_VMEM,
        out_shape=pltpu.VMEM(shape, one.dtype),
        compiler_params=PARAMS,
    )(*operands)


def partners(n, d):
    return [(i, i ^ d) for i in range(n)]


def after(value, *others):
    return lax.optimization_barrier((value,) + others)[0]


def swap(piece):
    return lax.ppermute(piece, "parts", partners(2, 1))


def any_line(held, mine, rest, spectra, exchange, lags_of):
    n_blk = lax.axis_size("blk")
    orders, parts = [], []
    for begin in range(0, n_blk, BATCH):
        order = tuple(range(begin, min(begin + BATCH, n_blk)))
        away = [d for d in order if d]
        arrived = [lax.ppermute(mine, "blk", partners(n_blk, d)) for d in away]
        known = [] if begin else [(spectra, 0, 0), (early_half(held, [(0, [rest])], 1), 0, 1)]
        known.append((early_half(held, [(d, [a]) for d, a in zip(away, arrived)], OWN), len(order) - len(away), OWN))
        parts += exchange(lags_of(known, [(d, [swap(a)]) for d, a in zip(away, arrived)], len(order)))
        orders.append(order)
    return orders, parts


def line_of_four(held, mine, theirs, arrived, near, rest, spectra, flipped, exchange, lags_of):
    middle = lax.ppermute(after(mine, spectra), "blk", [(0, 0), (1, 2), (2, 1), (3, 3)])
    arrived = [after(a, flipped) for a in arrived]
    ends = [lax.ppermute(a, "blk", partners(4, 1)) for a in arrived]
    second = join([after(arrived[0], near), *arrived[1:]])
    swapped = swap(second)
    pair = early_half(held, [(1, [near]), (2, [second])], OWN)
    rest_half = early_half(held, [(0, [after(rest, pair)])], 1)
    near_rest = lax.ppermute(after(theirs, rest_half), "blk", partners(4, 1))
    third = join(ends, middle)
    third_swapped = swap(third)
    known = [(spectra, 0, 0), (rest_half, 0, 1), (pair, 1, OWN), (early_half(held, [(3, [third])], OWN), 3, OWN)]
    late = [(1, [near_rest]), (2, [swapped]), (3, [third_swapped])]
    return [(0, 1, 2, 3)], exchange(lags_of(known, late, 4))


def shards(records, templates, masks, offsets):
    n_blk, n_chan, n_freq = (lax.axis_size(a) for a in ("blk", "chan", "freq"))
    windows = records.shape[0]
    blocks = n_chan * n_freq
    high, low = (jnp.asarray(t) for t in lag_tables())

    def exchange(found):
        return [found[0]] + [lax.ppermute(found[n], ("chan", "freq"), partners(blocks, n)) for n in range(1, blocks)]

    pieces = cut(templates, PIECES)
    mine = join(pieces)
    if n_blk == 4:
        arrived = [lax.ppermute(piece, "blk", partners(n_blk, 2)) for piece in pieces]
        near = lax.ppermute(mine, "blk", partners(n_blk, 1))
    held, spectra, theirs, rest = own_template(masks, offsets, records, templates, high, low)
    flipped = flip(held)
    after_all = (exchange, lambda *found: lag_blocks(held, flipped, *found, blocks))
    if n_blk == 4:
        orders, parts = line_of_four(held, mine, theirs, arrived, near, rest, spectra, flipped, *after_all)
    else:
        orders, parts = any_line(held, mine, rest, spectra, *after_all)
    return pl.pallas_call(
        functools.partial(sum_kernel, orders),
        in_specs=[IN_VMEM] * len(parts),
        out_specs=IN_VMEM,
        out_shape=jax.ShapeDtypeStruct((n_blk, windows, NSAMP // blocks), jnp.float32),
        compiler_params=PARAMS,
    )(*parts)


def solution(mesh):
    placed = (P(("parts", "blk"), None, "freq", "chan"), P("blk", None, "freq", "chan"), P(), P())
    return jax.shard_map(
        shards,
        mesh=mesh,
        in_specs=placed,
        out_specs=P(None, ("parts", "blk"), ("chan", "freq")),
        check_vma=False,
    )
```

```python
import functools
import math

import jax
import jax.numpy as jnp
import numpy as np
from jax import lax
from jax.experimental import pallas as pl
from jax.experimental.pallas import tpu as pltpu
from jax.sharding import PartitionSpec as P

NSAMP = 1024
BINS = 512
GROUP = 16
HALF = 128
RUN = 64
FOLD = 256
PIECES = 1
BATCH = 4
OWN, OTHER = 2, 3
VMEM_LIMIT = 24 * 2**20


def lag_tables():
    bins = np.arange(BINS).reshape(-1, HALF)
    angle = 2.0 * math.pi / NSAMP * (bins[..., None] * np.arange(FOLD) % NSAMP)
    table = math.sqrt(2.0 / BINS) * np.concatenate([np.cos(angle), -np.sin(angle)], axis=1)
    table = table.astype(np.float32)
    high = table.astype(jnp.bfloat16)
    low = (table - high.astype(np.float32)).astype(jnp.bfloat16)
    return high, low


def two_halves(values):
    high = values.astype(jnp.bfloat16)
    return high, (values - high.astype(jnp.float32)).astype(jnp.bfloat16)


def product(left, right, contract):
    return lax.dot_general(left, right, ((contract[:1], contract[1:]), ((), ())), preferred_element_type=jnp.float32)


def mask_row(masks, template_at, width):
    here = masks.shape[1] // lax.axis_size("chan")
    first = lax.axis_index("chan") * here
    lane = lax.broadcasted_iota(jnp.int32, (1, width), 1) // (width // here)
    row = jnp.zeros((1, width), jnp.float32)
    for b in range(here):
        row = jnp.where(lane == b, masks[template_at, first + b].astype(jnp.float32), row)
    return row


def block_transpose(values):
    row = lax.broadcasted_iota(jnp.int32, values.shape, 0)
    place = lax.broadcasted_iota(jnp.int32, values.shape, 1) // GROUP
    for bit in (1, 2, 4):
        up = pltpu.roll(pltpu.roll(values, 8 - bit, 0), bit * GROUP, 1)
        down = pltpu.roll(pltpu.roll(values, bit, 0), 8 * GROUP - bit * GROUP, 1)
        moved = jnp.where(row & bit == 0, up, down)
        values = jnp.where(row & bit == place & bit, values, moved)
    return values


def group_rows(records, half, g):
    bins = pl.ds(pl.multiple_of(half * HALF + g * GROUP, GROUP), GROUP)
    return jnp.concatenate(
        [jnp.concatenate([records[w, 0, bins, :], records[w, 1, bins, :]], axis=1) for w in range(records.shape[0])],
        axis=0,
    )


def flip_kernel(records, out):
    for g in range(HALF // GROUP):
        out[g] = group_rows(records, 1 - lax.axis_index("parts"), g).T


def half_spectra(entries, half, records, turn, used, ready=None, flipped=None):
    windows = records.shape[0]
    masks = [used[template_at].astype(jnp.bfloat16) for template_at, _ in entries]
    row = lax.broadcasted_iota(jnp.int32, (2 * GROUP * len(entries), windows * GROUP), 0)
    lane = lax.broadcasted_iota(jnp.int32, (2 * GROUP * len(entries), windows * GROUP), 1)
    same_bin = row % GROUP == lane % GROUP
    sums = [[] for _ in range(2 * len(entries))]
    for g in range(HALF // GROUP):
        if ready is not None:
            ready(g)
        weights = []
        for (_, pieces), mask in zip(entries, masks):
            piece = pieces[g * GROUP // pieces[0].shape[2]]
            start = g * GROUP % piece.shape[2]
            first, second = (piece[0, part, start : start + GROUP, :] * mask for part in range(2))
            weights.append(jnp.concatenate([first, second], axis=1))
            weights.append(jnp.concatenate([-second, first], axis=1))
        weights = jnp.concatenate(weights, axis=0)
        if flipped is None:
            every = product(weights, group_rows(records, half, g), (1, 1))
        else:
            every = product(weights, flipped[g], (1, 0))
        every = jnp.where(same_bin, every, 0.0)
        for i, found in enumerate(sums):
            found.append(jnp.sum(every[i * GROUP : (i + 1) * GROUP], axis=0, keepdims=True))
    wide = 8 * GROUP
    turned = []
    for i, (template_at, _) in enumerate(entries):
        real, imag = (
            jnp.concatenate(
                [block_transpose(found[:, at : at + wide]) for at in range(0, windows * GROUP, wide)], axis=0
            )
            for found in (jnp.concatenate(sums[2 * i + part], axis=0) for part in range(2))
        )
        cosine, sine_table = (turn[template_at, part, pl.ds(half, 1)] for part in range(2))
        turned.append((real * cosine - imag * sine_table, real * sine_table + imag * cosine))
    return turned


def half_lags(real, imag, high, low):
    windows = real.shape[0]
    straight = jnp.concatenate([real, imag], axis=1)
    turned = jnp.concatenate([imag, -real], axis=1)
    lane = lax.broadcasted_iota(jnp.int32, straight.shape, 1) % 4
    picked = [jnp.where(lane == r, straight, 0.0) for r in range(4)]
    picked += [jnp.where(lane == r, turned, 0.0) for r in (1, 3)]
    rows = jnp.concatenate(picked, axis=0)
    rows_high, rows_low = two_halves(rows)
    both = product(jnp.concatenate([rows_high, rows_low], axis=0), high, (1, 0))
    sums = both[: rows.shape[0]] + both[rows.shape[0] :] + product(rows_high, low, (1, 0))
    re0, re1, re2, re3, im1, im3 = (sums[i * windows : (i + 1) * windows] for i in range(6))
    even, odd, even_turned, odd_turned = re0 + re2, re1 + re3, re0 - re2, im1 - im3
    return jnp.concatenate([even + odd, even_turned - odd_turned, even - odd, even_turned + odd_turned], axis=1)


def own_kernel(
    masks, offsets, records, templates, high, low, held, turn, used, held_high, held_low, spectra, theirs, rest, template, numbers, sems
):
    halves = turn.shape[2]
    runs = records.shape[2] // RUN
    first_half = lax.axis_index("freq") * halves
    small = [
        pltpu.make_async_copy(masks, numbers[0], sems.at[0]),
        pltpu.make_async_copy(offsets, numbers[1], sems.at[1]),
    ]
    pieces = [
        pltpu.make_async_copy(values.at[:, :, pl.ds(r * RUN, RUN), :], to.at[:, :, pl.ds(r * RUN, RUN), :], sem)
        for r in range(runs)
        for values, to, sem in (
            (templates, template, sems.at[5 + 2 * r]),
            (records, held, sems.at[6 + 2 * r]),
        )
        if r < HALF // RUN or to is held
    ]
    tables = [
        pltpu.make_async_copy(table.at[pl.ds(first_half, halves)], to, sems.at[2 + i])
        for i, (table, to) in enumerate(((high, held_high), (low, held_low)))
    ]
    from_bin = pl.multiple_of((1 - lax.axis_index("parts")) * HALF, HALF)
    tables.append(pltpu.make_async_copy(templates.at[:, :, pl.ds(from_bin, HALF), :], theirs, sems.at[4]))
    tables.append(pltpu.make_async_copy(templates.at[:, :, pl.ds(HALF, rest.shape[2]), :], rest, sems.at[5 + 2 * runs]))
    for copy in small + pieces + tables:
        copy.start()
    for copy in small:
        copy.wait()
    masks, offsets = numbers
    row = lax.broadcasted_iota(jnp.int32, (halves, HALF), 0)
    lane = lax.broadcasted_iota(jnp.int32, (halves, HALF), 1)
    bin_index = (first_half + row) * HALF + lane
    for t in range(turn.shape[0]):
        phase = offsets[t] * bin_index % NSAMP
        angle = 2.0 * math.pi / NSAMP * phase.astype(jnp.float32)
        turn[t, 0] = jnp.cos(angle)
        turn[t, 1] = jnp.sin(angle)
        used[t] = mask_row(masks, t, held.shape[3])
    template_at = lax.axis_index("blk")

    def ready(g):
        if g * GROUP % RUN == 0:
            at = 2 * g * GROUP // RUN
            for copy in pieces[at : at + 2]:
                copy.wait()

    ((spectra[0, 0], spectra[0, 1]),) = half_spectra([(template_at, [template])], 0, held, turn, used, ready)
    for copy in pieces[2 * HALF // RUN :] + tables:
        copy.wait()


def half_at(place):
    part = lax.axis_index("parts")
    return {OWN: part, OTHER: 1 - part}.get(place, place)


def entries_of(ds, counts, refs):
    entries = []
    for d, count in zip(ds, counts):
        entries.append((lax.axis_index("blk") ^ d, refs[:count]))
        refs = refs[count:]
    return entries


def pieces_kernel(plan, held, turn, used, *refs):
    ds, counts, place = plan
    *refs, out = refs
    found = half_spectra(entries_of(ds, counts, refs), half_at(place), held, turn, used)
    for i, (real, imag) in enumerate(found):
        out[i, 0] = real
        out[i, 1] = imag


def early_lags_kernel(plan, held, turn, used, high, low, *refs):
    ds, counts, known, whole = plan
    *refs, out, spectra = refs
    for ref, (first, place) in zip(refs, known):
        for i in range(ref.shape[0]):
            spectra[first + i, half_at(place)] = ref[i]
    entries = entries_of(ds, counts, refs[len(known) :])
    found = half_spectra(entries, half_at(OWN), held, turn, used)
    total, windows = out.shape[:2]
    for i, (real, imag) in enumerate(found):
        at = total - len(entries) + i
        spectra[at, half_at(OWN), 0] = real
        spectra[at, half_at(OWN), 1] = imag
    for count, place in ((total, OWN), (whole, OTHER)):
        half = half_at(place)
        if count:
            real, imag = (jnp.concatenate([spectra[i, half, p] for i in range(count)], axis=0) for p in range(2))
            lags = half_lags(real, imag, high[half], low[half])
            for i in range(count):
                add = lags[i * windows : (i + 1) * windows]
                out[i] = add if place == OWN else out[i] + add


def lags_kernel(plan, held, turn, used, high, low, flipped, early, *refs):
    ds, counts = plan
    *refs, lags = refs
    blocks, windows, width = lags.shape
    outs = refs[-blocks:]
    entries = entries_of(ds, counts, refs[:-blocks])
    half = half_at(OTHER)
    found = half_spectra(entries, half, held, turn, used, flipped=flipped)
    real, imag = (jnp.concatenate([f[p] for f in found], axis=0) for p in range(2))
    late = half_lags(real, imag, high[half], low[half])
    me = lax.axis_index("chan") * lax.axis_size("freq") + lax.axis_index("freq")
    whole = early.shape[0] - len(entries)
    for i in range(early.shape[0]):
        for n in range(blocks):
            at = slice(n * width, (n + 1) * width)
            lags[n] = early[i, :, at]
            if i >= whole:
                lags[n] += late[(i - whole) * windows : (i - whole + 1) * windows, at]
        for n in range(blocks):
            outs[n][i] = lags[me ^ n]


def sum_kernel(orders, *refs):
    *parts, out = refs
    per = len(parts) // len(orders)
    for g, order in enumerate(orders):
        for i, d in enumerate(order):
            total = parts[g * per][i]
            for part in parts[g * per + 1 : (g + 1) * per]:
                total += part[i]
            out[lax.axis_index("blk") ^ d] = total


IN_VMEM = pl.BlockSpec(memory_space=pltpu.VMEM)
IN_HBM = pl.BlockSpec(memory_space=pltpu.HBM)
PARAMS = pltpu.CompilerParams(vmem_limit_bytes=VMEM_LIMIT)


def in_vmem(values):
    return [pltpu.with_memory_space_constraint(v, pltpu.VMEM) for v in values]


def in_hbm(values):
    return [pltpu.with_memory_space_constraint(v, pltpu.HBM) for v in values]


def own_template(masks, offsets, records, template, high, low):
    windows, _, bin_count, width = records.shape
    halves = bin_count // HALF
    table = (halves,) + high.shape[1:]
    out_shape = [
        pltpu.VMEM(records.shape, records.dtype),
        pltpu.VMEM((offsets.shape[0], 2, halves, HALF), jnp.float32),
        pltpu.VMEM((offsets.shape[0], 1, width), jnp.float32),
        pltpu.VMEM(table, high.dtype),
        pltpu.VMEM(table, low.dtype),
        pltpu.VMEM((1, 2, windows, HALF), jnp.float32),
        pltpu.VMEM((1, 2, HALF, width), template.dtype),
        pltpu.VMEM((1, 2, bin_count - HALF, width), template.dtype),
    ]
    *held, spectra, theirs, rest = pl.pallas_call(
        own_kernel,
        in_specs=[IN_HBM] * 6,
        out_specs=[IN_VMEM] * len(out_shape),
        out_shape=out_shape,
        scratch_shapes=[
            pltpu.VMEM((1, 2, HALF, width), template.dtype),
            (pltpu.SMEM(masks.shape, masks.dtype), pltpu.SMEM(offsets.shape, offsets.dtype)),
            pltpu.SemaphoreType.DMA((2 * (bin_count // RUN) + 6,)),
        ],
        compiler_params=PARAMS,
    )(*in_hbm((masks, offsets, records, template, high, low)))
    return held, spectra, theirs, rest


def early_half(held, entries, place):
    windows = held[0].shape[0]
    plan = (tuple(d for d, _ in entries), tuple(len(pieces) for _, pieces in entries), place)
    operands = in_vmem([*held[:3], *(piece for _, pieces in entries for piece in pieces)])
    return pl.pallas_call(
        functools.partial(pieces_kernel, plan),
        in_specs=[IN_VMEM] * len(operands),
        out_specs=IN_VMEM,
        out_shape=pltpu.VMEM((len(entries), 2, windows, HALF), jnp.float32),
        compiler_params=PARAMS,
    )(*operands)


def flip(held):
    windows, _, _, width = held[0].shape
    return pl.pallas_call(
        flip_kernel,
        in_specs=[IN_VMEM],
        out_specs=IN_VMEM,
        out_shape=pltpu.VMEM((HALF // GROUP, 2 * width, windows * GROUP), held[0].dtype),
        compiler_params=PARAMS,
    )(*in_vmem(held[:1]))


def early_lags(held, known, entries, count, whole):
    windows = held[0].shape[0]
    plan = (
        tuple(d for d, _ in entries),
        tuple(len(pieces) for _, pieces in entries),
        tuple((first, place) for _, first, place in known),
        whole,
    )
    operands = in_vmem([*held, *(k[0] for k in known), *(piece for _, pieces in entries for piece in pieces)])
    return pl.pallas_call(
        functools.partial(early_lags_kernel, plan),
        in_specs=[IN_VMEM] * len(operands),
        out_specs=IN_VMEM,
        out_shape=pltpu.VMEM((count, windows, NSAMP), jnp.float32),
        scratch_shapes=[pltpu.VMEM((count, held[0].shape[2] // HALF, 2, windows, HALF), jnp.float32)],
        compiler_params=PARAMS,
    )(*operands)


def lag_blocks(held, flipped, early, entries, blocks):
    count, windows, _ = early.shape
    block = (windows, NSAMP // blocks)
    plan = (tuple(d for d, _ in entries), tuple(len(pieces) for _, pieces in entries))
    operands = in_vmem([*held, flipped, early, *(piece for _, pieces in entries for piece in pieces)])
    return pl.pallas_call(
        functools.partial(lags_kernel, plan),
        in_specs=[IN_VMEM] * len(operands),
        out_specs=[IN_VMEM] * blocks,
        out_shape=[jax.ShapeDtypeStruct((count,) + block, jnp.float32)] * blocks,
        scratch_shapes=[pltpu.VMEM((blocks,) + block, jnp.float32)],
        compiler_params=PARAMS,
    )(*operands)


def cut_kernel(template, *rest):
    *outs, sems = rest
    at = lax.axis_index("parts") * sum(out.shape[2] for out in outs)
    copies = []
    for i, out in enumerate(outs):
        bins = pl.ds(pl.multiple_of(at, GROUP), out.shape[2])
        copies.append(pltpu.make_async_copy(template.at[:, :, bins, :], out, sems.at[i]))
        at += out.shape[2]
    for copy in copies:
        copy.start()
    for copy in copies:
        copy.wait()


def cut(template, count):
    shape = template.shape[:2] + (template.shape[2] // (2 * count),) + template.shape[3:]
    return pl.pallas_call(
        cut_kernel,
        in_specs=[IN_HBM],
        out_specs=[IN_VMEM] * count,
        out_shape=[pltpu.VMEM(shape, template.dtype)] * count,
        scratch_shapes=[pltpu.SemaphoreType.DMA((count,))],
        compiler_params=PARAMS,
    )(*in_hbm([template]))


def join_kernel(count, *refs):
    *pieces, out = refs
    width = pieces[0].shape[2]
    for i in range(count):
        out[:, :, i * width : (i + 1) * width, :] = pieces[i][...]
    if len(pieces) > count:

        @pl.when((lax.axis_index("blk") + 1) & 2 != 0)
        def _():
            out[...] = pieces[count][...]


def join(pieces, *middle):
    one = pieces[0]
    shape = one.shape[:2] + (len(pieces) * one.shape[2],) + one.shape[3:]
    operands = in_vmem([*pieces, *middle])
    return pl.pallas_call(
        functools.partial(join_kernel, len(pieces)),
        in_specs=[IN_VMEM] * len(operands),
        out_specs=IN_VMEM,
        out_shape=pltpu.VMEM(shape, one.dtype),
        compiler_params=PARAMS,
    )(*operands)


def partners(n, d):
    return [(i, i ^ d) for i in range(n)]


def after(value, *others):
    return lax.optimization_barrier((value,) + others)[0]


def swap(piece):
    return lax.ppermute(piece, "parts", partners(2, 1))


def any_line(held, mine, rest, spectra, exchange, lags_of):
    n_blk = lax.axis_size("blk")
    orders, parts = [], []
    for begin in range(0, n_blk, BATCH):
        order = tuple(range(begin, min(begin + BATCH, n_blk)))
        away = [d for d in order if d]
        arrived = [lax.ppermute(mine, "blk", partners(n_blk, d)) for d in away]
        known = [] if begin else [(spectra, 0, 0), (early_half(held, [(0, [rest])], 1), 0, 1)]
        whole = len(order) - len(away)
        early = early_lags(held, known, [(d, [a]) for d, a in zip(away, arrived)], len(order), whole)
        parts += exchange(lags_of(early, [(d, [swap(a)]) for d, a in zip(away, arrived)]))
        orders.append(order)
    return orders, parts


def line_of_four(held, mine, theirs, arrived, near, rest, spectra, flipped, exchange, lags_of):
    middle = lax.ppermute(after(mine, spectra), "blk", [(0, 0), (1, 2), (2, 1), (3, 3)])
    arrived = [after(a, flipped) for a in arrived]
    ends = [lax.ppermute(a, "blk", partners(4, 1)) for a in arrived]
    second = join([after(arrived[0], near), *arrived[1:]])
    swapped = swap(second)
    pair = early_half(held, [(1, [near]), (2, [second])], OWN)
    rest_half = early_half(held, [(0, [after(rest, pair)])], 1)
    near_rest = lax.ppermute(after(theirs, rest_half), "blk", partners(4, 1))
    third = join(ends, middle)
    third_swapped = swap(third)
    early = early_lags(held, [(spectra, 0, 0), (rest_half, 0, 1), (pair, 1, OWN)], [(3, [third])], 4, 1)
    late = [(1, [near_rest]), (2, [swapped]), (3, [third_swapped])]
    return [(0, 1, 2, 3)], exchange(lags_of(early, late))


def shards(records, templates, masks, offsets):
    n_blk, n_chan, n_freq = (lax.axis_size(a) for a in ("blk", "chan", "freq"))
    windows = records.shape[0]
    blocks = n_chan * n_freq
    high, low = (jnp.asarray(t) for t in lag_tables())

    def exchange(found):
        return [found[0]] + [lax.ppermute(found[n], ("chan", "freq"), partners(blocks, n)) for n in range(1, blocks)]

    pieces = cut(templates, PIECES)
    mine = join(pieces)
    if n_blk == 4:
        arrived = [lax.ppermute(piece, "blk", partners(n_blk, 2)) for piece in pieces]
        near = lax.ppermute(mine, "blk", partners(n_blk, 1))
    held, spectra, theirs, rest = own_template(masks, offsets, records, templates, high, low)
    flipped = flip(held)
    after_all = (exchange, lambda *found: lag_blocks(held, flipped, *found, blocks))
    if n_blk == 4:
        orders, parts = line_of_four(held, mine, theirs, arrived, near, rest, spectra, flipped, *after_all)
    else:
        orders, parts = any_line(held, mine, rest, spectra, *after_all)
    return pl.pallas_call(
        functools.partial(sum_kernel, orders),
        in_specs=[IN_VMEM] * len(parts),
        out_specs=IN_VMEM,
        out_shape=jax.ShapeDtypeStruct((n_blk, windows, NSAMP // blocks), jnp.float32),
        compiler_params=PARAMS,
    )(*parts)


def solution(mesh):
    placed = (P(("parts", "blk"), None, "freq", "chan"), P("blk", None, "freq", "chan"), P(), P())
    return jax.shard_map(
        shards,
        mesh=mesh,
        in_specs=placed,
        out_specs=P(None, ("parts", "blk"), ("chan", "freq")),
        check_vma=False,
    )
```
